256 devices in a mesh: replica: 8 (over z_lo, core), fsdp: 32 (over y, x, z_hi).
Axes of the slice: x: 4, y: 4, z: 8 (z_hi: 2, z_lo: 4; z = z_hi * 4 + z_lo), core: 2. Of those that a mesh axis runs over, the one named last changes fastest.
Arguments:
- activations: bfloat16 [8, 8192, 12288], P('replica', 'fsdp'), may hold values from -18 to 18
- norm_gain: bfloat16 [12288], replicated, may hold values from 0.25 to 1.75
- key_cotangent: bfloat16 [8, 8192, 512], P('replica', 'fsdp'), may hold values from -6 to 6
- key_weight: bfloat16 [8, 12288, 512], P('replica', 'fsdp'), may hold values from -6 to 6
- adam_first: float32 [8, 12288, 512], P('replica', 'fsdp'), may hold values from -6 to 6
- adam_second: float32 [8, 12288, 512], P('replica', 'fsdp'), may hold values from 0.05 to 1
- outer_codes: bfloat16 [8, 12288, 128], P('replica', 'fsdp'), may hold values from -127 to 127, as said below
- outer_scales: bfloat16 [8, 12288], P('replica', 'fsdp'), may hold values from 0.0009994507 to 0.0099487305
- global_fragment: float32 [12288, 128], P('fsdp'), may hold values from -6 to 6
- outer_momentum: float32 [12288, 128], P('fsdp'), may hold values from -4 to 4
- fragment_index: int32 [1], replicated, may hold values from 0 to 99999
Outputs:
- projected: bfloat16 [8, 8192, 512], P('replica', 'fsdp')
- new_weight: bfloat16 [8, 12288, 512], P('replica', 'fsdp')
- new_first: float32 [8, 12288, 512], P('replica', 'fsdp')
- new_second: float32 [8, 12288, 512], P('replica', 'fsdp')
- new_momentum: float32 [12288, 128], P('fsdp')
- new_global: float32 [12288, 128], P('fsdp')
The draws below stay inside these ranges and needn't reach their ends.
Inputs may be any that keep to these rules, and one draw needn't show every extreme that they name: `outer_codes`: whole numbers held as bfloat16.
All inputs are finite; a program needn't handle non-finite values.
Results may differ from the reference program's by a relative error of at most 0.018.
Values may be sent and summed in bfloat16 or wider, within the bound.
No kernel may reach another device: no remote copies, remote signals or barrier semaphores. Data moves between devices by JAX's collectives and lax.ppermute only.
A program may use at most 128 MiB of HBM per device.

```python
import math
import jax
import jax.numpy as jnp
from jax import lax

D = 12288
HEAD_DIM = 128
KV_HEADS = 4
TOK_DEV = 256
KEY_WIDTH = 512
TOKENS = 8192
N_REPLICA = 8
N_FSDP = 32


def draw_activations(key, part):
    key = jax.random.fold_in(key, 7)
    base_key, scale_key = jax.random.split(key)
    base = jnp.clip(jax.random.normal(base_key, (N_REPLICA, TOKENS, D), jnp.float32), -6.0, 6.0)
    spread = jnp.exp(jax.random.uniform(scale_key, (N_REPLICA, TOKENS, 1), jnp.float32, math.log(0.3), math.log(3.0)))
    return (base * spread).astype(jnp.bfloat16)


def draw_outer_codes(key, part):
    key = jax.random.fold_in(key, 11)
    values = jax.random.randint(key, (N_REPLICA, D, HEAD_DIM), -127, 128)
    return values.astype(jnp.float32).astype(jnp.bfloat16)


def steps_of(key, dims, pieces, least, largest):
    loudness, own = 1.0, jax.random.fold_in(key, 6)
    for position, parts in pieces:
        steps = jnp.exp(jax.random.uniform(jax.random.fold_in(own, position), (parts,), jnp.float32, least / len(pieces), largest / len(pieces)))
        loudness = loudness * jnp.repeat(steps, dims[position] // parts).reshape([-1 if axis == position else 1 for axis in range(len(dims))])
    return loudness


def noise(own_key, extent, width, reach, pieces=(), held_as=jnp.bfloat16):
    result = width * jax.random.normal(own_key, extent, jnp.float32)
    if pieces:
        result = result * steps_of(own_key, extent, pieces, -0.22, 0.18)
    return jnp.clip(result, -reach, reach).astype(held_as)


def setup_inputs(seed: int = 0) -> dict:
    key_list = jax.random.split(jax.random.key(seed), 12)
    activations = draw_activations(jax.random.fold_in(key_list[11], 71), 0)
    norm_gain = jnp.clip(1.0 + 0.15 * jax.random.normal(key_list[1], (D,), jnp.float32), 0.25, 1.75).astype(jnp.bfloat16)
    key_cotangent = noise(key_list[2], (N_REPLICA, TOKENS, KEY_WIDTH), 1.0, 6.0, ((0, 8), (1, 32)))
    key_weight = noise(key_list[3], (N_REPLICA, D, KEY_WIDTH), 1.0, 6.0, ((0, 8), (1, 32)))
    adam_first = noise(key_list[4], (N_REPLICA, D, KEY_WIDTH), 0.5, 6.0, ((0, 8), (1, 32)), jnp.float32)
    adam_second = jnp.clip(jnp.exp(math.log(1.0) - 2.9957323 * jax.random.uniform(key_list[5], (N_REPLICA, D, KEY_WIDTH), jnp.float32) ** steps_of(key_list[5], (N_REPLICA, D, KEY_WIDTH), ((0, 8), (1, 32)), -0.2, 0.2)), 0.05, 1.0)
    outer_codes = draw_outer_codes(jax.random.fold_in(key_list[11], 71), 0)
    outer_scales = jnp.clip(jnp.exp(math.log(0.0099487305) - 2.2979944 * jax.random.uniform(key_list[7], (N_REPLICA, D), jnp.float32) ** steps_of(key_list[7], (N_REPLICA, D), ((0, 8), (1, 32)), -0.2, 0.2)), 0.0009994507, 0.0099487305).astype(jnp.bfloat16)
    global_fragment = noise(key_list[8], (D, HEAD_DIM), 1.0, 6.0, ((0, 32),), jnp.float32)
    outer_momentum = noise(key_list[9], (D, HEAD_DIM), 0.3, 4.0, ((0, 32),), jnp.float32)
    fragment_index = jax.random.randint(key_list[10], (1,), 0, 100000).astype(jnp.int32)
    return dict(activations=activations, norm_gain=norm_gain, key_cotangent=key_cotangent, key_weight=key_weight, adam_first=adam_first, adam_second=adam_second, outer_codes=outer_codes, outer_scales=outer_scales, global_fragment=global_fragment, outer_momentum=outer_momentum, fragment_index=fragment_index)


norm_epsilon = 1e-05
adam_epsilon = 1e-08
beta_one = 0.9
beta_two = 0.95
inner_rate = 0.02
decay_rate = 0.1
outer_beta = 0.9
outer_rate = 0.7
mix_weight = 0.5

def normalize(token_rows, norm_gain):
    widened = token_rows.astype(jnp.float32)
    mean_square = lax.optimization_barrier(jnp.mean(widened * widened, axis=-1, keepdims=True))
    return (widened * lax.rsqrt(mean_square + norm_epsilon) * norm_gain.astype(jnp.float32)).astype(jnp.bfloat16)

def reference(activations, norm_gain, key_cotangent, key_weight, adam_first, adam_second, outer_codes, outer_scales, global_fragment, outer_momentum, fragment_index):
    factor = D ** (-0.5)
    outer_delta = lax.optimization_barrier(jnp.sum(outer_codes.astype(jnp.float32) * outer_scales.astype(jnp.float32)[:, :, None], axis=0)) / N_REPLICA
    new_momentum = outer_beta * outer_momentum + outer_delta
    new_global = global_fragment - outer_rate * (outer_delta + outer_beta * new_momentum)
    offset = (jnp.remainder(fragment_index[0], KV_HEADS) * HEAD_DIM).astype(jnp.int32)

    def replica_step(inputs):
        token_rows, cotangent, weight, moment_one, moment_two = inputs
        normed = normalize(token_rows, norm_gain)
        projected = (factor * jnp.dot(normed, weight, preferred_element_type=jnp.float32)).astype(jnp.bfloat16)
        grouped_rows = normed.reshape(N_FSDP, TOK_DEV, D)
        grouped_cot = cotangent.reshape(N_FSDP, TOK_DEV, KEY_WIDTH)

        def add_group(running, group_pair):
            left_side, right_side = group_pair
            partial_term = (factor * jnp.dot(left_side.T, right_side, preferred_element_type=jnp.float32)).astype(jnp.bfloat16)
            partial_term = lax.optimization_barrier(partial_term)
            return (running + partial_term.astype(jnp.float32), None)
        gradient, _ = lax.scan(add_group, jnp.zeros((D, KEY_WIDTH), jnp.float32), (grouped_rows, grouped_cot))
        first_new = beta_one * moment_one + (1.0 - beta_one) * gradient
        second_new = beta_two * moment_two + (1.0 - beta_two) * gradient * gradient
        master = weight.astype(jnp.float32)
        stepped = master - inner_rate * (first_new / (jnp.sqrt(second_new) + adam_epsilon) + decay_rate * master)
        current = lax.dynamic_slice_in_dim(stepped, offset, HEAD_DIM, 1)
        blended = mix_weight * current + (1.0 - mix_weight) * new_global
        merged = lax.dynamic_update_slice_in_dim(stepped, blended, offset, 1)
        return (projected, merged.astype(jnp.bfloat16), first_new, second_new)
    projected, new_weight, new_first, new_second = lax.map(replica_step, (activations, key_cotangent, key_weight, adam_first, adam_second))
    return (projected, new_weight, new_first, new_second, new_momentum, new_global)
```

```python
import functools

import jax
import jax.numpy as jnp
from jax import lax
from jax.experimental import pallas as pl
from jax.experimental.pallas import tpu as pltpu
from jax.sharding import PartitionSpec as P

norm_epsilon = 1e-05
adam_epsilon = 1e-08
beta_one = 0.9
beta_two = 0.95
inner_rate = 0.02
decay_rate = 0.1
outer_beta = 0.9
outer_rate = 0.7
mix_weight = 0.5

NY, NX, NZ = 4, 4, 2
ROWS = 32
VMEM_LIMIT = 48 * 1024 * 1024


def place(y, x, z):
    return ((y % NY) * NX + x % NX) * NZ + z % NZ


def shift(value, dy, dx, dz):
    pairs = [
        (place(y, x, z), place(y + dy, x + dx, z + dz))
        for y in range(NY)
        for x in range(NX)
        for z in range(NZ)
    ]
    return lax.ppermute(value, "fsdp", pairs)


def whole_blocks(count):
    return [pl.BlockSpec(memory_space=pltpu.VMEM)] * count


def norm_kernel(width, layout, column_ref, rows_ref, gain_ref, *outs):
    features = rows_ref.shape[1]
    rows = rows_ref.shape[0]

    def add_squares(step, total):
        part = rows_ref[:, pl.ds(pl.multiple_of(step * width, 128), width)].astype(jnp.float32)
        return total + part * part

    total = lax.fori_loop(
        0, features // width, add_squares, jnp.zeros((rows, width), jnp.float32), unroll=4
    )
    scale = lax.rsqrt(jnp.sum(total, axis=1, keepdims=True) / features + norm_epsilon)
    for out, blocks in zip(outs, layout):
        for position, block in enumerate(blocks):
            column = pl.multiple_of(column_ref[block], 128)
            part = rows_ref[:, pl.ds(column, width)].astype(jnp.float32)
            gain = gain_ref[:, pl.ds(column, width)]
            out[:, position * width : (position + 1) * width] = (part * scale * gain).astype(
                jnp.bfloat16
            )


def normalize(token_rows, gain, columns, layout, width):
    tokens, features = token_rows.shape
    return pl.pallas_call(
        functools.partial(norm_kernel, width, layout),
        grid_spec=pltpu.PrefetchScalarGridSpec(
            num_scalar_prefetch=1,
            grid=(tokens // ROWS,),
            in_specs=[
                pl.BlockSpec((ROWS, features), lambda i, c: (i, 0)),
                pl.BlockSpec((1, features), lambda i, c: (0, 0)),
            ],
            out_specs=[
                pl.BlockSpec((ROWS, width * len(blocks)), lambda i, c: (i, 0)) for blocks in layout
            ],
        ),
        out_shape=[
            jax.ShapeDtypeStruct((tokens, width * len(blocks)), jnp.bfloat16) for blocks in layout
        ],
        compiler_params=pltpu.CompilerParams(vmem_limit_bytes=VMEM_LIMIT),
        cost_estimate=pl.CostEstimate(
            flops=6 * tokens * features, bytes_accessed=4 * tokens * features, transcendentals=0
        ),
        name="norm",
    )(columns, token_rows, gain)


def gradient_kernel(sources, factor, *refs):
    cots, rows, outs = refs[:sources], refs[sources : 2 * sources], refs[2 * sources :]
    width = outs[0].shape[1]
    for j, out in enumerate(outs):
        total = None
        for cot, row in zip(cots, rows):
            term = jnp.dot(
                cot[...], row[:, j * width : (j + 1) * width], preferred_element_type=jnp.float32
            )
            total = term if total is None else total + term
        out[...] = (factor * total).astype(jnp.bfloat16)


def gradient_blocks(cots, rows, width, factor):
    count = rows[0].shape[1] // width
    keys, tokens = cots[0].shape
    work = len(cots) * keys * tokens * width * count
    return pl.pallas_call(
        functools.partial(gradient_kernel, len(cots), factor),
        in_specs=whole_blocks(2 * len(cots)),
        out_specs=whole_blocks(count),
        out_shape=[jax.ShapeDtypeStruct((keys, width), jnp.bfloat16)] * count,
        compiler_params=pltpu.CompilerParams(vmem_limit_bytes=VMEM_LIMIT),
        cost_estimate=pl.CostEstimate(
            flops=2 * work, bytes_accessed=8 * 2**20, transcendentals=0
        ),
        name="gradient",
    )(*cots, *rows)


def project_kernel(sources, pieces, factor, has_start, *refs):
    refs = list(refs)
    starts = [refs.pop(0) for _ in range(sources)] if has_start else [None] * sources
    rows = [[refs.pop(0) for _ in range(sources)] for _ in range(len(pieces))]
    weights = [refs.pop(0) for _ in range(len(refs) - sources)]
    outs = refs
    for source, (start, out) in enumerate(zip(starts, outs)):
        total = None if start is None else start[...]
        for group, blocks in zip(rows, pieces):
            for position, (weight, low, high) in enumerate(blocks):
                width = high - low
                term = jnp.dot(
                    group[source][:, position * width : (position + 1) * width],
                    weights[weight][low:high, :],
                    preferred_element_type=jnp.float32,
                )
                total = term if total is None else total + term
        if has_start:
            total = factor * total
        out[...] = total.astype(out.dtype)


def project(starts, rows, weights, pieces, out_types, factor):
    sources = len(rows[0])
    tokens = rows[0][0].shape[0]
    keys = weights[0].shape[1]
    depth = sum(group[0].shape[1] for group in rows)
    flat = list(starts or []) + [r for group in rows for r in group] + list(weights)
    return pl.pallas_call(
        functools.partial(project_kernel, sources, pieces, factor, starts is not None),
        in_specs=whole_blocks(len(flat)),
        out_specs=whole_blocks(sources),
        out_shape=[jax.ShapeDtypeStruct((tokens, keys), t) for t in out_types],
        compiler_params=pltpu.CompilerParams(vmem_limit_bytes=VMEM_LIMIT),
        cost_estimate=pl.CostEstimate(
            flops=2 * sources * tokens * keys * depth,
            bytes_accessed=8 * 2**20,
            transcendentals=0,
        ),
        name="project",
    )(*flat)


def update_kernel(
    offset_ref, own, one, two, three, far, weight, first, second, fresh, merged_out, first_out, second_out
):
    summed = own[...].astype(jnp.float32)
    for other in (one, two, three, far):
        summed = summed + other[...].astype(jnp.float32)
    gradient = summed.T
    moment_one = beta_one * first[...] + (1.0 - beta_one) * gradient
    moment_two = beta_two * second[...] + (1.0 - beta_two) * gradient * gradient
    first_out[...] = moment_one
    second_out[...] = moment_two
    master = weight[...].astype(jnp.float32)
    stepped = master - inner_rate * (
        moment_one / (jnp.sqrt(moment_two) + adam_epsilon) + decay_rate * master
    )
    head = fresh.shape[1]
    for position in range(master.shape[1] // head):
        part = stepped[:, position * head : (position + 1) * head]
        blended = mix_weight * part + (1.0 - mix_weight) * fresh[...]
        merged_out[:, position * head : (position + 1) * head] = jnp.where(
            offset_ref[0] == position, blended, part
        ).astype(jnp.bfloat16)


def update(head_index, terms, weight, first, second, fresh):
    rows, keys = weight.shape
    head = fresh.shape[1]
    block = 128
    return pl.pallas_call(
        update_kernel,
        grid_spec=pltpu.PrefetchScalarGridSpec(
            num_scalar_prefetch=1,
            grid=(rows // block,),
            in_specs=[pl.BlockSpec((keys, block), lambda i, o: (0, i))] * 5
            + [pl.BlockSpec((block, keys), lambda i, o: (i, 0))] * 3
            + [pl.BlockSpec((block, head), lambda i, o: (i, 0))],
            out_specs=[pl.BlockSpec((block, keys), lambda i, o: (i, 0))] * 3,
        ),
        out_shape=[
            jax.ShapeDtypeStruct((rows, keys), jnp.bfloat16),
            jax.ShapeDtypeStruct((rows, keys), jnp.float32),
            jax.ShapeDtypeStruct((rows, keys), jnp.float32),
        ],
        compiler_params=pltpu.CompilerParams(vmem_limit_bytes=VMEM_LIMIT),
        cost_estimate=pl.CostEstimate(
            flops=20 * rows * keys, bytes_accessed=6 * 2**20, transcendentals=0
        ),
        name="update",
    )(head_index, *terms, weight, first, second, fresh)


def per_device(
    activations,
    norm_gain,
    key_cotangent,
    key_weight,
    adam_first,
    adam_second,
    outer_codes,
    outer_scales,
    global_fragment,
    outer_momentum,
    fragment_index,
):
    token_rows = activations[0]
    weight_shard = key_weight[0]
    features = token_rows.shape[1]
    factor = features ** (-0.5)
    width = weight_shard.shape[0]
    replicas = lax.axis_size("replica")

    me = lax.axis_index("fsdp")
    my_y, my_x, my_z = me // (NX * NZ), (me // NZ) % NX, me % NZ

    cot = key_cotangent[0].T
    cots = [cot] + [shift(cot, 0, d, 0) for d in (1, 2, 3)]

    pair = jnp.concatenate([weight_shard, shift(weight_shard, 0, 0, 1)], axis=0)
    pairs = [pair] + [shift(pair, -e, 0, 0) for e in (1, 2, 3)]

    table = [(d, e, z) for d in range(NX) for e in range(NY) for z in range(NZ)]
    columns = jnp.stack(
        [
            ((((my_y + e) % NY) * NX + (my_x + d) % NX) * NZ + (my_z + z) % NZ) * width
            for d, e, z in table
        ]
    ).astype(jnp.int32)
    at = {key: number for number, key in enumerate(table)}
    far_z = [[at[d, e, 1] for e in range(NY)] for d in range(NX)]
    near_z = [[at[d, e, 0] for e in range(1, NY)] for d in range(NX)]
    own_z = [[at[d, 0, 0]] for d in range(NX)]
    parts = normalize(
        token_rows,
        norm_gain.astype(jnp.float32)[None],
        columns,
        far_z + near_z + own_z,
        width,
    )
    chunks = [parts[0:NX], parts[NX : 2 * NX], parts[2 * NX :]]
    chunks = [[c[0]] + [shift(c[d], 0, d, 0) for d in (1, 2, 3)] for c in chunks]

    far = gradient_blocks(cots, chunks[0], width, factor)
    far = [far[0]] + [shift(far[e], e, 0, 0) for e in (1, 2, 3)]
    far = sum(f.astype(jnp.float32) for f in far).astype(jnp.bfloat16)
    far = shift(far, 0, 0, 1)
    near = gradient_blocks(cots, chunks[1], width, factor)
    near = [shift(near[e - 1], e, 0, 0) for e in (1, 2, 3)]
    own = gradient_blocks(cots, chunks[2], width, factor)

    early = project(
        None,
        chunks[:2],
        pairs,
        [
            [(e, width, 2 * width) for e in range(NY)],
            [(e, 0, width) for e in range(1, NY)],
        ],
        [jnp.float32] * NX,
        factor,
    )
    late = project(
        early,
        chunks[2:],
        [weight_shard],
        [[(0, 0, width)]],
        [jnp.float32] + [jnp.bfloat16] * (NX - 1),
        factor,
    )
    back = [shift(late[d], 0, -d, 0) for d in (1, 2, 3)]
    projected = (late[0] + sum(b.astype(jnp.float32) for b in back)).astype(jnp.bfloat16)

    delta = outer_codes[0].astype(jnp.float32) * outer_scales[0].astype(jnp.float32)[:, None]
    step = 1
    while step < replicas:
        delta = delta + lax.ppermute(
            delta, "replica", [(r, r ^ step) for r in range(replicas)]
        )
        step *= 2
    outer_delta = delta / replicas
    momentum = outer_beta * outer_momentum + outer_delta
    refreshed = global_fragment - outer_rate * (outer_delta + outer_beta * momentum)

    heads = weight_shard.shape[1] // global_fragment.shape[1]
    head_index = jnp.remainder(fragment_index, heads).astype(jnp.int32)
    merged, moment_one, moment_two = update(
        head_index,
        list(own) + near + [far],
        weight_shard,
        adam_first[0],
        adam_second[0],
        refreshed,
    )
    return (
        projected[None],
        merged[None],
        moment_one[None],
        moment_two[None],
        momentum,
        refreshed,
    )


def solution(mesh):
    in_specs = (
        P("replica", "fsdp", None),
        P(),
        P("replica", "fsdp", None),
        P("replica", "fsdp", None),
        P("replica", "fsdp", None),
        P("replica", "fsdp", None),
        P("replica", "fsdp", None),
        P("replica", "fsdp"),
        P("fsdp", None),
        P("fsdp", None),
        P(),
    )
    out_specs = (
        P("replica", "fsdp", None),
        P("replica", "fsdp", None),
        P("replica", "fsdp", None),
        P("replica", "fsdp", None),
        P("fsdp", None),
        P("fsdp", None),
    )
    return jax.shard_map(
        per_device, mesh=mesh, in_specs=in_specs, out_specs=out_specs, check_vma=False
    )
```

```python
import functools

import jax
import jax.numpy as jnp
from jax import lax
from jax.experimental import pallas as pl
from jax.experimental.pallas import tpu as pltpu
from jax.sharding import PartitionSpec as P

norm_epsilon = 1e-05
adam_epsilon = 1e-08
beta_one = 0.9
beta_two = 0.95
inner_rate = 0.02
decay_rate = 0.1
outer_beta = 0.9
outer_rate = 0.7
mix_weight = 0.5

NY, NX, NZ = 4, 4, 2
ROWS = 32
VMEM_LIMIT = 60 * 1024 * 1024


def place(y, x, z):
    return ((y % NY) * NX + x % NX) * NZ + z % NZ


def shift(value, dy, dx, dz):
    pairs = [
        (place(y, x, z), place(y + dy, x + dx, z + dz))
        for y in range(NY)
        for x in range(NX)
        for z in range(NZ)
    ]
    return lax.ppermute(value, "fsdp", pairs)


def in_memory(count):
    return [pl.BlockSpec(memory_space=pl.ANY)] * count


def call_options(work=1, limit=VMEM_LIMIT):
    return dict(
        compiler_params=pltpu.CompilerParams(vmem_limit_bytes=limit),
        cost_estimate=pl.CostEstimate(flops=work, bytes_accessed=1, transcendentals=0),
    )


def norm_kernel(width, blocks, extra, column_ref, rows_hbm, gain_ref, cot_hbm, *refs):
    outs, (held, ready, cot, came, gone, cot_came, cot_gone) = refs[:-7], refs[-7:]
    tokens, features = held.shape
    depth = width * len(blocks)
    lanes = 128
    bands = tokens // ROWS

    def fetch(band):
        rows = pl.ds(pl.multiple_of(band * ROWS, ROWS), ROWS)
        return pltpu.make_async_copy(rows_hbm.at[rows], held.at[rows], came.at[band])

    def store(band, x):
        rows = pl.ds(pl.multiple_of(band * ROWS, ROWS), ROWS)
        if len(outs) == 1:
            target = outs[0].at[x, rows, pl.ds(0, depth)]
        else:
            target = outs[x].at[rows]
        return pltpu.make_async_copy(ready.at[x, rows], target, gone.at[band, x])

    for band in range(bands):
        fetch(band).start()
    cot_copies = []
    if extra:
        cot_fetch = pltpu.make_async_copy(cot_hbm, cot, cot_came)
        cot_fetch.start()
        cot_copies = [
            pltpu.make_async_copy(cot, outs[0].at[x, :, pl.ds(depth, extra)], cot_gone.at[x])
            for x in range(NX)
        ]
    columns = [column_ref[number] for number in range(NX * len(blocks))]
    if extra:
        cot_fetch.wait()
        for copy in cot_copies:
            copy.start()

    @pl.loop(0, bands)
    def _(band):
        fetch(band).wait()
        rows = pl.ds(pl.multiple_of(band * ROWS, ROWS), ROWS)
        sums = [jnp.zeros((ROWS, lanes), jnp.float32) for _ in range(2)]
        for k in range(features // lanes):
            part = held[rows, k * lanes : (k + 1) * lanes].astype(jnp.float32)
            sums[k % 2] = sums[k % 2] + part * part
        total = jnp.sum(sums[0] + sums[1], axis=1, keepdims=True)
        scale = lax.rsqrt(total / features + norm_epsilon)
        scale = jnp.broadcast_to(scale, (ROWS, lanes))
        for x in range(NX):
            for position in range(len(blocks)):
                start = columns[x * len(blocks) + position]
                for k in range(0, width, lanes):
                    column = pl.multiple_of(start + k, lanes)
                    part = held[rows, pl.ds(column, lanes)].astype(jnp.float32)
                    gain = gain_ref[:, pl.ds(column, lanes)]
                    low = position * width + k
                    ready[x, rows, low : low + lanes] = (part * scale * gain).astype(jnp.bfloat16)
            store(band, x).start()

    for copy in cot_copies:
        copy.wait()
    for band in range(bands):
        for x in range(NX):
            store(band, x).wait()


def normalize(token_rows, gain, cot, columns, blocks, width, extra, work):
    tokens, features = token_rows.shape
    depth = width * len(blocks)
    bands = tokens // ROWS
    if extra:
        out_shape = [jax.ShapeDtypeStruct((NX, tokens, depth + extra), jnp.bfloat16)]
    else:
        out_shape = [jax.ShapeDtypeStruct((tokens, depth), jnp.bfloat16)] * NX
    return pl.pallas_call(
        functools.partial(norm_kernel, width, blocks, extra),
        in_specs=[
            pl.BlockSpec(memory_space=pltpu.SMEM),
            pl.BlockSpec(memory_space=pl.ANY),
            pl.BlockSpec(memory_space=pltpu.VMEM),
            pl.BlockSpec(memory_space=pl.ANY),
        ],
        out_specs=in_memory(len(out_shape)),
        out_shape=out_shape,
        scratch_shapes=[
            pltpu.VMEM((tokens, features), jnp.bfloat16),
            pltpu.VMEM((NX, tokens, depth), jnp.bfloat16),
            pltpu.VMEM(cot.shape, jnp.bfloat16),
            pltpu.SemaphoreType.DMA((bands,)),
            pltpu.SemaphoreType.DMA((bands, NX)),
            pltpu.SemaphoreType.DMA,
            pltpu.SemaphoreType.DMA((NX,)),
        ],
        name="norm",
        **call_options(work),
    )(columns, token_rows, gain, cot)


def gradient_kernel(factor, width, count, skip, turn, sources_ref, cots_hbm, *refs):
    rows_count = 1 if turn else NX
    rows_hbm, refs = refs[:rows_count], refs[rows_count:]
    outs, refs = refs[: count - NY + 2], refs[count - NY + 2 :]
    cots, rows, ready, raw, cots_came, came, gone, turned_gone = refs
    sources, tokens, keys = raw.shape
    fetches, stores = [], []
    if turn:
        cots_copy = pltpu.make_async_copy(
            cots_hbm.at[:, :, pl.ds(count * width, keys)], raw, cots_came
        )
    else:
        cots_copy = pltpu.make_async_copy(cots_hbm, cots, cots_came)
    cots_copy.start()
    for j in range(count):
        span = pl.ds((skip + j) * width, width)
        if turn:
            pieces = [pltpu.make_async_copy(rows_hbm[0].at[:, :, span], rows.at[j], came.at[j, 0])]
        else:
            pieces = [
                pltpu.make_async_copy(
                    rows_hbm[s].at[:, span], rows.at[j, sources_ref[s]], came.at[j, s]
                )
                for s in range(sources)
            ]
        fetches.append(pieces)
        target = outs[0].at[sources_ref[j]] if j < NY else outs[1 + j - NY]
        stores.append(pltpu.make_async_copy(ready.at[j], target, gone.at[j]))
        for piece in pieces:
            piece.start()
    cots_copy.wait()
    if turn:
        for source in range(sources):
            cots[:, source * tokens : (source + 1) * tokens] = raw[source].T
        turned_copy = pltpu.make_async_copy(cots, outs[-1], turned_gone)
        turned_copy.start()
        stores.append(turned_copy)
    for j in range(count):
        for piece in fetches[j]:
            piece.wait()
        total = jnp.dot(
            cots[...],
            rows[j].reshape(sources * tokens, width),
            preferred_element_type=jnp.float32,
        )
        ready[j] = (factor * total).astype(jnp.bfloat16)
        stores[j].start()
    for store in stores:
        store.wait()


def gradient_blocks(
    sources, cots, rows, keys, width, factor, turn, work, skip=0, count=None
):
    tokens = rows[0].shape[-2]
    if count is None:
        count = (rows[0].shape[-1] - (keys if turn else 0)) // width - skip
    out_shape = [jax.ShapeDtypeStruct((NY, keys, width), jnp.bfloat16)]
    out_shape += [jax.ShapeDtypeStruct((keys, width), jnp.bfloat16)] * (count - NY)
    if turn:
        out_shape.append(jax.ShapeDtypeStruct((keys, NX * tokens), jnp.bfloat16))
    return pl.pallas_call(
        functools.partial(gradient_kernel, factor, width, count, skip, turn),
        in_specs=[pl.BlockSpec(memory_space=pltpu.SMEM)] + in_memory(1 + len(rows)),
        out_specs=in_memory(len(out_shape)),
        out_shape=out_shape,
        scratch_shapes=[
            pltpu.VMEM((keys, NX * tokens), jnp.bfloat16),
            pltpu.VMEM((count, NX, tokens, width), jnp.bfloat16),
            pltpu.VMEM((count, keys, width), jnp.bfloat16),
            pltpu.VMEM((NX, tokens, keys), jnp.bfloat16),
            pltpu.SemaphoreType.DMA,
            pltpu.SemaphoreType.DMA((count, NX)),
            pltpu.SemaphoreType.DMA((count,)),
            pltpu.SemaphoreType.DMA,
        ],
        name="gradient",
        **call_options(work),
    )(sources, cots, *rows)


def project_kernel(factor, count, has_start, sources_ref, *refs):
    refs = list(refs)
    start_hbm = refs.pop(0) if has_start else None
    rows_hbm = [refs.pop(0) for _ in range(NX if has_start else 1)]
    weights_hbm = [refs.pop(0) for _ in range(count)]
    out_hbm, rows, weights, ready, start, weights_came, came, gone, start_came = refs
    sources = rows.shape[0]
    width = weights.shape[0] // count
    weight_copies = [
        pltpu.make_async_copy(
            weights_hbm[j], weights.at[pl.ds(j * width, width)], weights_came.at[j]
        )
        for j in range(count)
    ]
    fetches, stores, starts = [], [], []
    for s in range(sources):
        if has_start:
            fetches.append(pltpu.make_async_copy(rows_hbm[s], rows.at[s], came.at[s]))
            place_at = sources_ref[s]
            starts.append(
                pltpu.make_async_copy(start_hbm.at[place_at], start.at[s], start_came.at[s])
            )
        else:
            span = pl.ds(0, count * width)
            fetches.append(
                pltpu.make_async_copy(rows_hbm[0].at[s, :, span], rows.at[s], came.at[s])
            )
            place_at = s
        stores.append(pltpu.make_async_copy(ready.at[s], out_hbm.at[place_at], gone.at[s]))
    for copy in weight_copies + fetches + starts:
        copy.start()
    for copy in weight_copies:
        copy.wait()
    for s in range(sources):
        fetches[s].wait()
        total = jnp.dot(rows[s], weights[...], preferred_element_type=jnp.float32)
        if has_start:
            starts[s].wait()
            total = factor * (total + start[s])
        ready[s] = total.astype(ready.dtype)
        stores[s].start()
    for store in stores:
        store.wait()


def project(sources, start, rows, weights, out_type, factor):
    tokens = rows[0].shape[-2]
    width, keys = weights[0].shape
    count = len(weights)
    has_start = start is not None
    flat = ([start] if has_start else []) + list(rows) + list(weights)
    return pl.pallas_call(
        functools.partial(project_kernel, factor, count, has_start),
        in_specs=[pl.BlockSpec(memory_space=pltpu.SMEM)] + in_memory(len(flat)),
        out_specs=pl.BlockSpec(memory_space=pl.ANY),
        out_shape=jax.ShapeDtypeStruct((NX, tokens, keys), out_type),
        scratch_shapes=[
            pltpu.VMEM((NX, tokens, count * width), jnp.bfloat16),
            pltpu.VMEM((count * width, keys), jnp.bfloat16),
            pltpu.VMEM((NX, tokens, keys), out_type),
            pltpu.VMEM((NX, tokens, keys), jnp.float32),
            pltpu.SemaphoreType.DMA((count,)),
            pltpu.SemaphoreType.DMA((NX,)),
            pltpu.SemaphoreType.DMA((NX,)),
            pltpu.SemaphoreType.DMA((NX,)),
        ],
        name="project",
        **call_options(),
    )(sources, *flat)


def near_gradient_kernel(factor, width, skip, sources_ref, cots, *refs):
    rows, outs = refs[:NX], refs[NX:]
    keys, all_tokens = cots.shape
    tokens = all_tokens // NX
    for j, out in enumerate(outs):
        span = slice((skip + j) * width, (skip + j + 1) * width)
        total = None
        for number, row in enumerate(rows):
            left = cots[:, pl.ds(pl.multiple_of(sources_ref[number] * tokens, 128), tokens)]
            term = jnp.dot(left, row[:, span], preferred_element_type=jnp.float32)
            total = term if total is None else total + term
        out[...] = (factor * total).astype(jnp.bfloat16)


def near_gradient(sources, cots, rows, width, factor, skip, count, work):
    keys = cots.shape[0]
    vmem = pl.BlockSpec(memory_space=pltpu.VMEM)
    return pl.pallas_call(
        functools.partial(near_gradient_kernel, factor, width, skip),
        in_specs=[pl.BlockSpec(memory_space=pltpu.SMEM)] + [vmem] * (1 + NX),
        out_specs=[vmem] * count,
        out_shape=[jax.ShapeDtypeStruct((keys, width), jnp.bfloat16)] * count,
        name="near_gradient",
        **call_options(work, VMEM_LIMIT // 2),
    )(sources, cots, *rows)


def near_project_kernel(factor, sources_ref, start, *refs):
    rows, weights, out = refs[:NX], refs[NX:-1], refs[-1]
    width = weights[0].shape[0]
    for number, row in enumerate(rows):
        total = start[sources_ref[number]]
        for j, weight in enumerate(weights):
            total = total + jnp.dot(
                row[:, j * width : (j + 1) * width],
                weight[...],
                preferred_element_type=jnp.float32,
            )
        out[sources_ref[number]] = (factor * total).astype(jnp.bfloat16)


def near_project(sources, start, rows, weights, factor):
    vmem = pl.BlockSpec(memory_space=pltpu.VMEM)
    return pl.pallas_call(
        functools.partial(near_project_kernel, factor),
        in_specs=[pl.BlockSpec(memory_space=pltpu.SMEM)] + [vmem] * (1 + NX + len(weights)),
        out_specs=vmem,
        out_shape=jax.ShapeDtypeStruct(start.shape, jnp.bfloat16),
        name="near_project",
        **call_options(1, VMEM_LIMIT // 2),
    )(sources, start, *rows, *weights)


def update_kernel(
    offset_ref, own, one, two, three, far, weight, first, second, fresh, merged_out, first_out, second_out
):
    summed = own[...].astype(jnp.float32)
    for other in (one, two, three, far):
        summed = summed + other[...].astype(jnp.float32)
    gradient = summed.T
    moment_one = beta_one * first[...] + (1.0 - beta_one) * gradient
    moment_two = beta_two * second[...] + (1.0 - beta_two) * gradient * gradient
    first_out[...] = moment_one
    second_out[...] = moment_two
    master = weight[...].astype(jnp.float32)
    stepped = master - inner_rate * (
        moment_one / (jnp.sqrt(moment_two) + adam_epsilon) + decay_rate * master
    )
    head = fresh.shape[1]
    for position in range(master.shape[1] // head):
        part = stepped[:, position * head : (position + 1) * head]
        blended = mix_weight * part + (1.0 - mix_weight) * fresh[...]
        merged_out[:, position * head : (position + 1) * head] = jnp.where(
            offset_ref[0] == position, blended, part
        ).astype(jnp.bfloat16)


def update(head_index, terms, weight, first, second, fresh):
    rows, keys = weight.shape
    head = fresh.shape[1]
    block = 128
    return pl.pallas_call(
        update_kernel,
        grid_spec=pltpu.PrefetchScalarGridSpec(
            num_scalar_prefetch=1,
            grid=(rows // block,),
            in_specs=[pl.BlockSpec((keys, block), lambda i, o: (0, i))] * 5
            + [pl.BlockSpec((block, keys), lambda i, o: (i, 0))] * 3
            + [pl.BlockSpec((block, head), lambda i, o: (i, 0))],
            out_specs=[pl.BlockSpec((block, keys), lambda i, o: (i, 0))] * 3,
        ),
        out_shape=[
            jax.ShapeDtypeStruct((rows, keys), jnp.bfloat16),
            jax.ShapeDtypeStruct((rows, keys), jnp.float32),
            jax.ShapeDtypeStruct((rows, keys), jnp.float32),
        ],
        name="update",
        **call_options(limit=VMEM_LIMIT // 4),
    )(head_index, *terms, weight, first, second, fresh)


def per_device(
    activations,
    norm_gain,
    key_cotangent,
    key_weight,
    adam_first,
    adam_second,
    outer_codes,
    outer_scales,
    global_fragment,
    outer_momentum,
    fragment_index,
):
    token_rows = activations[0]
    weight_shard = key_weight[0]
    features = token_rows.shape[1]
    factor = features ** (-0.5)
    width = weight_shard.shape[0]
    replicas = lax.axis_size("replica")

    def swap_x(value):
        return lax.all_to_all(value, "fsdp", 0, 0, axis_index_groups=along_x, tiled=True)

    def add_replica(value, step):
        return value + lax.ppermute(value, "replica", [(r, r ^ step) for r in range(replicas)])

    me = lax.axis_index("fsdp")
    my_y, my_x, my_z = me // (NX * NZ), (me // NZ) % NX, me % NZ

    along_y = [[place(y, x, z) for y in range(NY)] for x in range(NX) for z in range(NZ)]
    along_x = [[place(y, x, z) for x in range(NX)] for y in range(NY) for z in range(NZ)]

    def swap_x(value):
        return lax.all_to_all(value, "fsdp", 0, 0, axis_index_groups=along_x, tiled=True)

    def swap_x(value):
        return lax.all_to_all(value, "fsdp", 0, 0, axis_index_groups=along_x, tiled=True)

    def columns_of(relative_x, blocks):
        return jnp.stack(
            [
                place(my_y + y, (0 if relative_x is None else my_x) + x, my_z + z) * width
                for x in range(NX)
                for y, z in blocks
            ]
        ).astype(jnp.int32)

    gain = norm_gain.astype(jnp.float32)[None]
    cot = key_cotangent[0]
    keys = cot.shape[1]
    sources = jnp.stack([(my_x - d) % NX for d in range(NX)]).astype(jnp.int32)
    heavy = 10**11

    blocks = [(0, 1), (1, 1), (2, 1), (3, 1), (2, 0)]
    (part_one,) = normalize(
        token_rows, gain, cot, columns_of(None, blocks), blocks, width, keys, 1
    )
    chunk_one = swap_x(part_one)

    near_weights = [weight_shard] + [shift(weight_shard, -e, 0, 0) for e in range(1, NY)]
    far_weight = shift(weight_shard, 0, 0, 1)
    delta = outer_codes[0].astype(jnp.float32) * outer_scales[0].astype(jnp.float32)[:, None]
    delta = add_replica(delta, 1)
    delta = add_replica(delta, 2)

    token_rows, far_weight, near_weights = lax.optimization_barrier(
        (token_rows, far_weight, near_weights)
    )
    blocks = [(1, 0), (3, 0), (0, 0)]
    part_two = normalize(
        token_rows, gain, cot, columns_of(my_x, blocks), blocks, width, 0, 1
    )
    far_weights = [far_weight] + [shift(far_weight, -e, 0, 0) for e in range(1, NY)]
    delta = add_replica(delta, 4)
    part_two, far_weights, delta = lax.optimization_barrier((part_two, far_weights, delta))
    chunk_two = [part_two[0]] + [shift(part_two[d], 0, d, 0) for d in range(1, NX)]
    chunk_one, _ = lax.optimization_barrier((chunk_one, part_two))

    targets = jnp.stack([(my_y + e) % NY for e in range(NY)]).astype(jnp.int32)
    *first, cots = gradient_blocks(
        targets, chunk_one, [chunk_one], keys, width, factor, True, heavy
    )
    far = lax.all_to_all(first[0], "fsdp", 0, 0, axis_index_groups=along_y, tiled=True)
    near_two = shift(first[1], 2, 0, 0)
    partial = project(
        sources, None, [chunk_one], far_weights + [near_weights[2]], jnp.float32, factor
    )
    far = jnp.sum(far.astype(jnp.float32), axis=0).astype(jnp.bfloat16)
    cots, far, delta, partial = lax.optimization_barrier((cots, far, delta, partial))
    far = shift(far, 0, 0, 1)
    second = near_gradient(sources, cots, chunk_two, width, factor, 0, 2, heavy)
    near_one = shift(second[0], 1, 0, 0)
    near_three = shift(second[1], 3, 0, 0)

    partial, _ = lax.optimization_barrier((partial, second[1]))
    partial = near_project(
        sources, partial, chunk_two, [near_weights[1], near_weights[3], weight_shard], factor
    )
    partial, cots, far = lax.optimization_barrier((partial, cots, far))
    (own,) = near_gradient(sources, cots, chunk_two, width, factor, 2, 1, heavy)
    terms = [own, near_one, near_two, near_three, far]
    back = swap_x(partial)
    projected = jnp.sum(back.astype(jnp.float32), axis=0).astype(jnp.bfloat16)

    outer_delta = delta / replicas
    momentum = outer_beta * outer_momentum + outer_delta
    refreshed = global_fragment - outer_rate * (outer_delta + outer_beta * momentum)

    heads = weight_shard.shape[1] // global_fragment.shape[1]
    head_index = jnp.remainder(fragment_index, heads).astype(jnp.int32)
    merged, moment_one, moment_two = update(
        head_index,
        terms,
        weight_shard,
        adam_first[0],
        adam_second[0],
        refreshed,
    )
    return (
        projected[None],
        merged[None],
        moment_one[None],
        moment_two[None],
        momentum,
        refreshed,
    )


def solution(mesh):
    in_specs = (
        P("replica", "fsdp", None),
        P(),
        P("replica", "fsdp", None),
        P("replica", "fsdp", None),
        P("replica", "fsdp", None),
        P("replica", "fsdp", None),
        P("replica", "fsdp", None),
        P("replica", "fsdp"),
        P("fsdp", None),
        P("fsdp", None),
        P(),
    )
    out_specs = (
        P("replica", "fsdp", None),
        P("replica", "fsdp", None),
        P("replica", "fsdp", None),
        P("replica", "fsdp", None),
        P("fsdp", None),
        P("fsdp", None),
    )
    return jax.shard_map(
        per_device, mesh=mesh, in_specs=in_specs, out_specs=out_specs, check_vma=False
    )
```

```python
import functools

import jax
import jax.numpy as jnp
from jax import lax
from jax.experimental import pallas as pl
from jax.experimental.pallas import tpu as pltpu
from jax.sharding import PartitionSpec as P

norm_epsilon = 1e-05
adam_epsilon = 1e-08
beta_one = 0.9
beta_two = 0.95
inner_rate = 0.02
decay_rate = 0.1
outer_beta = 0.9
outer_rate = 0.7
mix_weight = 0.5

NY, NX, NZ = 4, 4, 2
ROWS = 32
AHEAD = 3
VMEM_LIMIT = 60 * 1024 * 1024
HEAVY = 10**11


def place(y, x, z):
    return ((y % NY) * NX + x % NX) * NZ + z % NZ


def shift(value, dy, dx, dz):
    pairs = [
        (place(y, x, z), place(y + dy, x + dx, z + dz))
        for y in range(NY)
        for x in range(NX)
        for z in range(NZ)
    ]
    return lax.ppermute(value, "fsdp", pairs)


def in_memory(count):
    return [pl.BlockSpec(memory_space=pl.ANY)] * count


def call_options(work=1, limit=VMEM_LIMIT):
    return dict(
        compiler_params=pltpu.CompilerParams(vmem_limit_bytes=limit),
        cost_estimate=pl.CostEstimate(flops=work, bytes_accessed=1, transcendentals=0),
    )


def norm_kernel(width, blocks, relative, extra, rows_hbm, gain_ref, cot_hbm, *refs):
    outs, (held, ready, cot, gains, came, gone, cot_came, cot_gone) = refs[:-8], refs[-8:]
    tokens, features = held.shape
    depth = width * len(blocks)
    lanes = 128
    bands = tokens // ROWS
    me = lax.axis_index("fsdp")
    my_y, my_x, my_z = me // (NX * NZ), (me // NZ) % NX, me % NZ

    def fetch(band):
        rows = pl.ds(pl.multiple_of(band * ROWS, ROWS), ROWS)
        return pltpu.make_async_copy(rows_hbm.at[rows], held.at[rows], came.at[band])

    def store(band, x):
        rows = pl.ds(pl.multiple_of(band * ROWS, ROWS), ROWS)
        if len(outs) == 1:
            target = outs[0].at[x, rows, pl.ds(0, depth)]
        else:
            target = outs[x].at[rows]
        return pltpu.make_async_copy(ready.at[x, rows], target, gone.at[band, x])

    for band in range(AHEAD):
        fetch(band).start()
    cot_copies = []
    if extra:
        cot_fetch = pltpu.make_async_copy(cot_hbm, cot, cot_came)
        cot_fetch.start()
        cot_copies = [
            pltpu.make_async_copy(cot, outs[0].at[x, :, pl.ds(depth, extra)], cot_gone.at[x])
            for x in range(NX)
        ]
    gains[...] = gain_ref[...].astype(jnp.float32)
    starts = [
        [
            place(my_y + y, (my_x if relative else 0) + x, my_z + z) * (width // lanes)
            for y, z in blocks
        ]
        for x in range(NX)
    ]

    @pl.loop(0, bands)
    def _(band):
        @pl.when(band + AHEAD < bands)
        def _():
            fetch(band + AHEAD).start()

        fetch(band).wait()
        rows = pl.ds(pl.multiple_of(band * ROWS, ROWS), ROWS)
        sums = [jnp.zeros((ROWS, lanes), jnp.float32) for _ in range(2)]
        for k in range(features // lanes):
            part = held[rows, k * lanes : (k + 1) * lanes].astype(jnp.float32)
            sums[k % 2] = sums[k % 2] + part * part
        total = jnp.sum(sums[0] + sums[1], axis=1, keepdims=True)
        scale = lax.rsqrt(total / features + norm_epsilon)
        scale = jnp.broadcast_to(scale, (ROWS, lanes))
        for x in range(NX):
            for position in range(len(blocks)):
                for k in range(width // lanes):
                    tile = starts[x][position] + k
                    column = pl.multiple_of(tile * lanes, lanes)
                    part = held[rows, pl.ds(column, lanes)].astype(jnp.float32)
                    gain = gains[pl.ds(tile, 1), :]
                    low = position * width + k * lanes
                    ready[x, rows, low : low + lanes] = (part * scale * gain).astype(jnp.bfloat16)
            store(band, x).start()

    if extra:
        cot_fetch.wait()
        for copy in cot_copies:
            copy.start()
        for copy in cot_copies:
            copy.wait()
    for band in range(bands):
        for x in range(NX):
            store(band, x).wait()


def normalize(token_rows, gain, cot, blocks, relative, width, extra):
    tokens, features = token_rows.shape
    depth = width * len(blocks)
    bands = tokens // ROWS
    if extra:
        out_shape = [jax.ShapeDtypeStruct((NX, tokens, depth + extra), jnp.bfloat16)]
    else:
        out_shape = [jax.ShapeDtypeStruct((tokens, depth), jnp.bfloat16)] * NX
    return pl.pallas_call(
        functools.partial(norm_kernel, width, blocks, relative, extra),
        in_specs=[
            pl.BlockSpec(memory_space=pl.ANY),
            pl.BlockSpec(memory_space=pltpu.VMEM),
            pl.BlockSpec(memory_space=pl.ANY),
        ],
        out_specs=in_memory(len(out_shape)),
        out_shape=out_shape,
        scratch_shapes=[
            pltpu.VMEM((tokens, features), jnp.bfloat16),
            pltpu.VMEM((NX, tokens, depth), jnp.bfloat16),
            pltpu.VMEM(cot.shape, jnp.bfloat16),
            pltpu.VMEM(gain.shape, jnp.float32),
            pltpu.SemaphoreType.DMA((bands,)),
            pltpu.SemaphoreType.DMA((bands, NX)),
            pltpu.SemaphoreType.DMA,
            pltpu.SemaphoreType.DMA((NX,)),
        ],
        name="norm",
        **call_options(),
    )(token_rows, gain, cot)


VMEM = pl.BlockSpec(memory_space=pltpu.VMEM)
SMEM = pl.BlockSpec(memory_space=pltpu.SMEM)


def far_gradient_kernel(factor, width, targets_ref, chunk, far_hbm, cots, ready, gone):
    sources, tokens, depth = chunk.shape
    keys = cots.shape[0]
    for source in range(sources):
        cots[:, source * tokens : (source + 1) * tokens] = chunk[source, :, depth - keys :].T
    copies = []
    for j in range(NY):
        total = None
        for source in range(sources):
            term = jnp.dot(
                cots[:, source * tokens : (source + 1) * tokens],
                chunk[source, :, j * width : (j + 1) * width],
                preferred_element_type=jnp.float32,
            )
            total = term if total is None else total + term
        ready[j] = (factor * total).astype(jnp.bfloat16)
        copies.append(
            pltpu.make_async_copy(ready.at[j], far_hbm.at[targets_ref[j]], gone.at[j])
        )
        copies[j].start()
    for copy in copies:
        copy.wait()


def far_gradient(targets, chunk, keys, width, factor):
    sources, tokens, _ = chunk.shape
    return pl.pallas_call(
        functools.partial(far_gradient_kernel, factor, width),
        in_specs=[SMEM, VMEM],
        out_specs=[pl.BlockSpec(memory_space=pl.ANY), VMEM],
        out_shape=[
            jax.ShapeDtypeStruct((NY, keys, width), jnp.bfloat16),
            jax.ShapeDtypeStruct((keys, sources * tokens), jnp.bfloat16),
        ],
        scratch_shapes=[
            pltpu.VMEM((NY, keys, width), jnp.bfloat16),
            pltpu.SemaphoreType.DMA((NY,)),
        ],
        name="far_gradient",
        **call_options(HEAVY, VMEM_LIMIT // 3),
    )(targets, chunk)


def add_up_kernel(terms, out):
    total = terms[0].astype(jnp.float32)
    for number in range(1, terms.shape[0]):
        total = total + terms[number].astype(jnp.float32)
    out[...] = total.astype(out.dtype)


def add_up(terms):
    return pl.pallas_call(
        add_up_kernel,
        in_specs=[VMEM],
        out_specs=VMEM,
        out_shape=jax.ShapeDtypeStruct(terms.shape[1:], terms.dtype),
        name="add_up",
        **call_options(1, VMEM_LIMIT // 3),
    )(terms)


def far_project_kernel(sources_ref, chunk, *refs):
    weights, outs = refs[:-NX], refs[-NX:]
    width = weights[0].shape[0]
    for out_number, out in enumerate(outs):
        total = None
        for j, weight in enumerate(weights):
            term = jnp.dot(
                chunk[sources_ref[out_number], :, j * width : (j + 1) * width],
                weight[...],
                preferred_element_type=jnp.float32,
            )
            total = term if total is None else total + term
        out[...] = total


def far_project(sources, chunk, weights):
    count, tokens, _ = chunk.shape
    keys = weights[0].shape[1]
    return pl.pallas_call(
        far_project_kernel,
        in_specs=[SMEM] + [VMEM] * (1 + len(weights)),
        out_specs=[VMEM] * count,
        out_shape=[jax.ShapeDtypeStruct((tokens, keys), jnp.float32)] * count,
        name="far_project",
        **call_options(HEAVY, VMEM_LIMIT // 3),
    )(sources, chunk, *weights)


def near_gradient_kernel(factor, width, skip, sources_ref, cots, *refs):
    rows, outs = refs[:NX], refs[NX:]
    keys, all_tokens = cots.shape
    tokens = all_tokens // NX
    for j, out in enumerate(outs):
        span = slice((skip + j) * width, (skip + j + 1) * width)
        total = None
        for number, row in enumerate(rows):
            left = cots[:, pl.ds(pl.multiple_of(sources_ref[number] * tokens, 128), tokens)]
            term = jnp.dot(left, row[:, span], preferred_element_type=jnp.float32)
            total = term if total is None else total + term
        out[...] = (factor * total).astype(jnp.bfloat16)


def near_gradient(sources, cots, rows, width, factor, skip, count):
    keys = cots.shape[0]
    vmem = pl.BlockSpec(memory_space=pltpu.VMEM)
    return pl.pallas_call(
        functools.partial(near_gradient_kernel, factor, width, skip),
        in_specs=[pl.BlockSpec(memory_space=pltpu.SMEM)] + [vmem] * (1 + NX),
        out_specs=[vmem] * count,
        out_shape=[jax.ShapeDtypeStruct((keys, width), jnp.bfloat16)] * count,
        name="near_gradient",
        **call_options(HEAVY, VMEM_LIMIT // 3),
    )(sources, cots, *rows)


def near_project_kernel(factor, count, *refs):
    starts, rows, refs = refs[:count], refs[count : 2 * count], refs[2 * count :]
    weights, outs = refs[:-count], refs[-count:]
    width = weights[0].shape[0]
    for start, row, out in zip(starts, rows, outs):
        total = start[...]
        for j, weight in enumerate(weights):
            total = total + jnp.dot(
                row[:, j * width : (j + 1) * width],
                weight[...],
                preferred_element_type=jnp.float32,
            )
        out[...] = (factor * total).astype(out.dtype)


def near_project(starts, rows, weights, out_types, factor):
    count = len(rows)
    return pl.pallas_call(
        functools.partial(near_project_kernel, factor, count),
        in_specs=[VMEM] * (2 * count + len(weights)),
        out_specs=[VMEM] * count,
        out_shape=[jax.ShapeDtypeStruct(starts[0].shape, t) for t in out_types],
        name="near_project",
        **call_options(1, VMEM_LIMIT // 3),
    )(*starts, *rows, *weights)


def update_kernel(
    offset_ref, own, one, two, three, far, weight, first, second, fresh, merged_out, first_out, second_out
):
    summed = own[...].astype(jnp.float32)
    for other in (one, two, three, far):
        summed = summed + other[...].astype(jnp.float32)
    gradient = summed.T
    moment_one = beta_one * first[...] + (1.0 - beta_one) * gradient
    moment_two = beta_two * second[...] + (1.0 - beta_two) * gradient * gradient
    first_out[...] = moment_one
    second_out[...] = moment_two
    master = weight[...].astype(jnp.float32)
    stepped = master - inner_rate * (
        moment_one / (jnp.sqrt(moment_two) + adam_epsilon) + decay_rate * master
    )
    head = fresh.shape[1]
    for position in range(master.shape[1] // head):
        part = stepped[:, position * head : (position + 1) * head]
        blended = mix_weight * part + (1.0 - mix_weight) * fresh[...]
        merged_out[:, position * head : (position + 1) * head] = jnp.where(
            offset_ref[0] == position, blended, part
        ).astype(jnp.bfloat16)


def update(head_index, terms, weight, first, second, fresh):
    rows, keys = weight.shape
    head = fresh.shape[1]
    block = 128
    return pl.pallas_call(
        update_kernel,
        grid_spec=pltpu.PrefetchScalarGridSpec(
            num_scalar_prefetch=1,
            grid=(rows // block,),
            in_specs=[pl.BlockSpec((keys, block), lambda i, o: (0, i))] * 5
            + [pl.BlockSpec((block, keys), lambda i, o: (i, 0))] * 3
            + [pl.BlockSpec((block, head), lambda i, o: (i, 0))],
            out_specs=[pl.BlockSpec((block, keys), lambda i, o: (i, 0))] * 3,
        ),
        out_shape=[
            jax.ShapeDtypeStruct((rows, keys), jnp.bfloat16),
            jax.ShapeDtypeStruct((rows, keys), jnp.float32),
            jax.ShapeDtypeStruct((rows, keys), jnp.float32),
        ],
        name="update",
        **call_options(limit=VMEM_LIMIT // 4),
    )(head_index, *terms, weight, first, second, fresh)


def per_device(
    activations,
    norm_gain,
    key_cotangent,
    key_weight,
    adam_first,
    adam_second,
    outer_codes,
    outer_scales,
    global_fragment,
    outer_momentum,
    fragment_index,
):
    token_rows = activations[0]
    weight_shard = key_weight[0]
    features = token_rows.shape[1]
    factor = features ** (-0.5)
    width = weight_shard.shape[0]
    replicas = lax.axis_size("replica")

    def swap_x(value):
        return lax.all_to_all(value, "fsdp", 0, 0, axis_index_groups=along_x, tiled=True)

    def add_replica(value, step):
        return value + lax.ppermute(value, "replica", [(r, r ^ step) for r in range(replicas)])

    me = lax.axis_index("fsdp")
    my_y, my_x, my_z = me // (NX * NZ), (me // NZ) % NX, me % NZ

    along_y = [[place(y, x, z) for y in range(NY)] for x in range(NX) for z in range(NZ)]
    along_x = [[place(y, x, z) for x in range(NX)] for y in range(NY) for z in range(NZ)]

    def swap_x(value):
        return lax.all_to_all(value, "fsdp", 0, 0, axis_index_groups=along_x, tiled=True)

    def swap_x(value):
        return lax.all_to_all(value, "fsdp", 0, 0, axis_index_groups=along_x, tiled=True)

    gain = norm_gain.reshape(-1, 128)
    cot = key_cotangent[0]
    keys = cot.shape[1]
    sources = jnp.stack([(my_x - d) % NX for d in range(NX)]).astype(jnp.int32)
    targets = jnp.stack([(my_y + e) % NY for e in range(NY)]).astype(jnp.int32)

    blocks = [(e, 1) for e in range(NY)]
    (part_one,) = normalize(token_rows, gain, cot, blocks, False, width, keys)
    chunk_one = swap_x(part_one)

    near_weights = [weight_shard] + [shift(weight_shard, -e, 0, 0) for e in range(1, NY)]
    far_weight = shift(weight_shard, 0, 0, 1)
    delta = outer_codes[0].astype(jnp.float32) * outer_scales[0].astype(jnp.float32)[:, None]
    delta = add_replica(delta, 1)

    token_rows, far_weight, delta, near_weights = lax.optimization_barrier(
        (token_rows, far_weight, delta, near_weights)
    )
    blocks = [(1, 0), (2, 0), (3, 0), (0, 0)]
    part_two = normalize(token_rows, gain, cot, blocks, True, width, 0)
    far_weights = [far_weight] + [shift(far_weight, -e, 0, 0) for e in range(1, NY)]
    delta = add_replica(add_replica(delta, 2), 4)
    chunk_two = [part_two[0]] + [shift(part_two[d], 0, d, 0) for d in range(1, NX)]
    chunk_one, part_two, far_weights, delta = lax.optimization_barrier(
        (chunk_one, part_two, far_weights, delta)
    )

    far, cots = far_gradient(targets, chunk_one, keys, width, factor)
    far = lax.all_to_all(far, "fsdp", 0, 0, axis_index_groups=along_y, tiled=True)
    partial = far_project(sources, chunk_one, far_weights)
    far = add_up(far)
    cots, far, partial = lax.optimization_barrier((cots, far, partial))
    far = shift(far, 0, 0, 1)
    second = near_gradient(sources, cots, chunk_two, width, factor, 0, 3)
    near = [shift(second[e - 1], e, 0, 0) for e in range(1, NY)]

    weights = near_weights[1:] + [weight_shard]
    (back_two,) = near_project([partial[2]], [chunk_two[2]], weights, [jnp.bfloat16], factor)
    back_two = shift(back_two, 0, -2, 0)
    rest, _ = lax.optimization_barrier(([partial[d] for d in (0, 1, 3)], second))
    own_part, back_one, back_three = near_project(
        rest,
        [chunk_two[d] for d in (0, 1, 3)],
        weights,
        [jnp.float32, jnp.bfloat16, jnp.bfloat16],
        factor,
    )
    cots, far, own_part, _ = lax.optimization_barrier((cots, far, own_part, back_one))
    (own,) = near_gradient(sources, cots, chunk_two, width, factor, 3, 1)
    terms = [own] + near + [far]
    back = [back_two, shift(back_one, 0, -1, 0), shift(back_three, 0, -3, 0)]
    projected = (own_part + sum(b.astype(jnp.float32) for b in back)).astype(jnp.bfloat16)

    outer_delta = delta / replicas
    momentum = outer_beta * outer_momentum + outer_delta
    refreshed = global_fragment - outer_rate * (outer_delta + outer_beta * momentum)

    heads = weight_shard.shape[1] // global_fragment.shape[1]
    head_index = jnp.remainder(fragment_index, heads).astype(jnp.int32)
    merged, moment_one, moment_two = update(
        head_index,
        terms,
        weight_shard,
        adam_first[0],
        adam_second[0],
        refreshed,
    )
    return (
        projected[None],
        merged[None],
        moment_one[None],
        moment_two[None],
        momentum,
        refreshed,
    )


def solution(mesh):
    in_specs = (
        P("replica", "fsdp", None),
        P(),
        P("replica", "fsdp", None),
        P("replica", "fsdp", None),
        P("replica", "fsdp", None),
        P("replica", "fsdp", None),
        P("replica", "fsdp", None),
        P("replica", "fsdp"),
        P("fsdp", None),
        P("fsdp", None),
        P(),
    )
    out_specs = (
        P("replica", "fsdp", None),
        P("replica", "fsdp", None),
        P("replica", "fsdp", None),
        P("replica", "fsdp", None),
        P("fsdp", None),
        P("fsdp", None),
    )
    return jax.shard_map(
        per_device, mesh=mesh, in_specs=in_specs, out_specs=out_specs, check_vma=False
    )
```

```python
import functools

import jax
import jax.numpy as jnp
from jax import lax
from jax.experimental import pallas as pl
from jax.experimental.pallas import tpu as pltpu
from jax.sharding import PartitionSpec as P

norm_epsilon = 1e-05
adam_epsilon = 1e-08
beta_one = 0.9
beta_two = 0.95
inner_rate = 0.02
decay_rate = 0.1
outer_beta = 0.9
outer_rate = 0.7
mix_weight = 0.5

NY, NX, NZ = 4, 4, 2
ROWS = 32
AHEAD = 3
VMEM_LIMIT = 60 * 1024 * 1024
HEAVY = 10**11


def place(y, x, z):
    return ((y % NY) * NX + x % NX) * NZ + z % NZ


def shift(value, dy, dx, dz):
    pairs = [
        (place(y, x, z), place(y + dy, x + dx, z + dz))
        for y in range(NY)
        for x in range(NX)
        for z in range(NZ)
    ]
    return lax.ppermute(value, "fsdp", pairs)


def in_memory(count):
    return [pl.BlockSpec(memory_space=pl.ANY)] * count


def call_options(work=1, limit=VMEM_LIMIT):
    return dict(
        compiler_params=pltpu.CompilerParams(vmem_limit_bytes=limit),
        cost_estimate=pl.CostEstimate(flops=work, bytes_accessed=1, transcendentals=0),
    )


def norm_kernel(width, groups, relative, extra, rows_hbm, gain_ref, cot_hbm, *refs):
    outs, (held, ready, cot, gains, came, gone, cot_came, cot_gone) = refs[:-8], refs[-8:]
    tokens, features = held.shape
    blocks = [block for group in groups for block in group]
    lanes = 128
    bands = tokens // ROWS
    me = lax.axis_index("fsdp")
    my_y, my_x, my_z = me // (NX * NZ), (me // NZ) % NX, me % NZ

    def fetch(band):
        rows = pl.ds(pl.multiple_of(band * ROWS, ROWS), ROWS)
        return pltpu.make_async_copy(rows_hbm.at[rows], held.at[rows], came.at[band])

    def stores(band, x):
        rows = pl.ds(pl.multiple_of(band * ROWS, ROWS), ROWS)
        low, copies = 0, []
        for number, group in enumerate(groups):
            span = pl.ds(low, width * len(group))
            if relative:
                target = outs[number * NX + x].at[rows]
            else:
                target = outs[number].at[x, rows, span]
            copies.append(
                pltpu.make_async_copy(ready.at[x, rows, span], target, gone.at[band, x, number])
            )
            low += width * len(group)
        return copies

    for band in range(AHEAD):
        fetch(band).start()
    cot_copies = []
    if extra:
        cot_fetch = pltpu.make_async_copy(cot_hbm, cot, cot_came)
        cot_fetch.start()
        cot_copies = [
            pltpu.make_async_copy(cot, outs[0].at[x, :, pl.ds(width * len(blocks), extra)], cot_gone.at[x])
            for x in range(NX)
        ]
    gains[...] = gain_ref[...].astype(jnp.float32)
    starts = [
        [
            place(my_y + y, (my_x if relative else 0) + x, my_z + z) * (width // lanes)
            for y, z in blocks
        ]
        for x in range(NX)
    ]

    @pl.loop(0, bands)
    def _(band):
        @pl.when(band + AHEAD < bands)
        def _():
            fetch(band + AHEAD).start()

        fetch(band).wait()
        rows = pl.ds(pl.multiple_of(band * ROWS, ROWS), ROWS)
        sums = [jnp.zeros((ROWS, lanes), jnp.float32) for _ in range(2)]
        for k in range(features // lanes):
            part = held[rows, k * lanes : (k + 1) * lanes].astype(jnp.float32)
            sums[k % 2] = sums[k % 2] + part * part
        total = jnp.sum(sums[0] + sums[1], axis=1, keepdims=True)
        scale = lax.rsqrt(total / features + norm_epsilon)
        scale = jnp.broadcast_to(scale, (ROWS, lanes))
        for x in range(NX):
            for position in range(len(blocks)):
                for k in range(width // lanes):
                    tile = starts[x][position] + k
                    column = pl.multiple_of(tile * lanes, lanes)
                    part = held[rows, pl.ds(column, lanes)].astype(jnp.float32)
                    gain = gains[pl.ds(tile, 1), :]
                    low = position * width + k * lanes
                    ready[x, rows, low : low + lanes] = (part * scale * gain).astype(jnp.bfloat16)
            for copy in stores(band, x):
                copy.start()

    if extra:
        cot_fetch.wait()
        for copy in cot_copies:
            copy.start()
        for copy in cot_copies:
            copy.wait()
    for band in range(bands):
        for x in range(NX):
            for copy in stores(band, x):
                copy.wait()


def normalize(token_rows, gain, cot, groups, relative, width, extra):
    tokens, features = token_rows.shape
    depths = [width * len(group) for group in groups]
    bands = tokens // ROWS
    if relative:
        out_shape = [
            jax.ShapeDtypeStruct((tokens, depth), jnp.bfloat16) for depth in depths for _ in range(NX)
        ]
    else:
        out_shape = [jax.ShapeDtypeStruct((NX, tokens, depths[0] + extra), jnp.bfloat16)]
    return pl.pallas_call(
        functools.partial(norm_kernel, width, groups, relative, extra),
        in_specs=[
            pl.BlockSpec(memory_space=pl.ANY),
            pl.BlockSpec(memory_space=pltpu.VMEM),
            pl.BlockSpec(memory_space=pl.ANY),
        ],
        out_specs=in_memory(len(out_shape)),
        out_shape=out_shape,
        scratch_shapes=[
            pltpu.VMEM((tokens, features), jnp.bfloat16),
            pltpu.VMEM((NX, tokens, sum(depths)), jnp.bfloat16),
            pltpu.VMEM(cot.shape, jnp.bfloat16),
            pltpu.VMEM(gain.shape, jnp.float32),
            pltpu.SemaphoreType.DMA((bands,)),
            pltpu.SemaphoreType.DMA((bands, NX, len(groups))),
            pltpu.SemaphoreType.DMA,
            pltpu.SemaphoreType.DMA((NX,)),
        ],
        name="norm",
        **call_options(),
    )(token_rows, gain, cot)


VMEM = pl.BlockSpec(memory_space=pltpu.VMEM)
SMEM = pl.BlockSpec(memory_space=pltpu.SMEM)


def far_gradient_kernel(factor, width, targets_ref, chunk, far_hbm, cots, ready, gone):
    sources, tokens, depth = chunk.shape
    keys = cots.shape[0]
    for source in range(sources):
        cots[:, source * tokens : (source + 1) * tokens] = chunk[source, :, depth - keys :].T
    copies = []
    for j in range(NY):
        total = None
        for source in range(sources):
            term = jnp.dot(
                cots[:, source * tokens : (source + 1) * tokens],
                chunk[source, :, j * width : (j + 1) * width],
                preferred_element_type=jnp.float32,
            )
            total = term if total is None else total + term
        ready[j] = (factor * total).astype(jnp.bfloat16)
        copies.append(
            pltpu.make_async_copy(ready.at[j], far_hbm.at[targets_ref[j]], gone.at[j])
        )
        copies[j].start()
    for copy in copies:
        copy.wait()


def far_gradient(targets, chunk, keys, width, factor):
    sources, tokens, _ = chunk.shape
    return pl.pallas_call(
        functools.partial(far_gradient_kernel, factor, width),
        in_specs=[SMEM, VMEM],
        out_specs=[pl.BlockSpec(memory_space=pl.ANY), VMEM],
        out_shape=[
            jax.ShapeDtypeStruct((NY, keys, width), jnp.bfloat16),
            jax.ShapeDtypeStruct((keys, sources * tokens), jnp.bfloat16),
        ],
        scratch_shapes=[
            pltpu.VMEM((NY, keys, width), jnp.bfloat16),
            pltpu.SemaphoreType.DMA((NY,)),
        ],
        name="far_gradient",
        **call_options(HEAVY, VMEM_LIMIT // 3),
    )(targets, chunk)


def add_up_kernel(terms, out):
    total = terms[0].astype(jnp.float32)
    for number in range(1, terms.shape[0]):
        total = total + terms[number].astype(jnp.float32)
    out[...] = total.astype(out.dtype)


def add_up(terms):
    return pl.pallas_call(
        add_up_kernel,
        in_specs=[VMEM],
        out_specs=VMEM,
        out_shape=jax.ShapeDtypeStruct(terms.shape[1:], terms.dtype),
        name="add_up",
        **call_options(1, VMEM_LIMIT // 3),
    )(terms)


def fetch_weights(weights_hbm, weights, came):
    width = weights.shape[0] // len(weights_hbm)
    copies = [
        pltpu.make_async_copy(weight, weights.at[pl.ds(j * width, width)], came.at[j])
        for j, weight in enumerate(weights_hbm)
    ]
    for copy in copies:
        copy.start()
    return copies


def far_project_kernel(sources_ref, chunk, *refs):
    weights_hbm, (out, weights, came, ready, gone) = refs[:-5], refs[-5:]
    for copy in fetch_weights(weights_hbm, weights, came):
        copy.wait()
    copies = []
    for d in range(NX):
        ready[d] = jnp.dot(
            chunk[sources_ref[d], :, : weights.shape[0]],
            weights[...],
            preferred_element_type=jnp.float32,
        )
        copies.append(pltpu.make_async_copy(ready.at[d], out.at[d], gone.at[d]))
        copies[d].start()
    for copy in copies:
        copy.wait()


def far_project(sources, chunk, weights):
    count, tokens, _ = chunk.shape
    width, keys = weights[0].shape
    shape = (count, tokens, keys)
    return pl.pallas_call(
        far_project_kernel,
        in_specs=[SMEM, VMEM] + in_memory(len(weights)),
        out_specs=pl.BlockSpec(memory_space=pl.ANY),
        out_shape=jax.ShapeDtypeStruct(shape, jnp.float32),
        scratch_shapes=[
            pltpu.VMEM((width * len(weights), keys), jnp.bfloat16),
            pltpu.SemaphoreType.DMA((len(weights),)),
            pltpu.VMEM(shape, jnp.float32),
            pltpu.SemaphoreType.DMA((count,)),
        ],
        name="far_project",
        **call_options(HEAVY, VMEM_LIMIT // 3),
    )(sources, chunk, *weights)


def near_project_kernel(factor, pieces, start_hbm, *refs):
    rows_hbm, own_hbm, refs = refs[:NX], refs[NX : 2 * NX], refs[2 * NX :]
    weights_hbm, refs = refs[:pieces], refs[pieces:]
    outs, (weights, came, start, rows, start_came, rows_came) = refs[:NX], refs[NX:]
    depth = rows_hbm[0].shape[1]
    own_depth = own_hbm[0].shape[1]
    copies = fetch_weights(weights_hbm, weights, came)
    fetches = []
    for d in range(NX):
        fetches.append(
            [
                pltpu.make_async_copy(
                    rows_hbm[d], rows.at[d, :, pl.ds(0, depth)], rows_came.at[d, 0]
                ),
                pltpu.make_async_copy(
                    own_hbm[d], rows.at[d, :, pl.ds(depth, own_depth)], rows_came.at[d, 1]
                ),
                pltpu.make_async_copy(start_hbm.at[d], start.at[d], start_came.at[d]),
            ]
        )
        for copy in fetches[d]:
            copy.start()
    for copy in copies:
        copy.wait()
    for d in range(NX):
        for copy in fetches[d]:
            copy.wait()
        total = start[d] + jnp.dot(rows[d], weights[...], preferred_element_type=jnp.float32)
        outs[d][...] = (factor * total).astype(outs[d].dtype)


def near_project(start, rows, own_rows, weights, out_types, factor):
    width, keys = weights[0].shape
    count, tokens, _ = start.shape
    depth = width * len(weights)
    return pl.pallas_call(
        functools.partial(near_project_kernel, factor, len(weights)),
        in_specs=in_memory(1 + 2 * NX + len(weights)),
        out_specs=[VMEM] * NX,
        out_shape=[jax.ShapeDtypeStruct((tokens, keys), t) for t in out_types],
        scratch_shapes=[
            pltpu.VMEM((depth, keys), jnp.bfloat16),
            pltpu.SemaphoreType.DMA((len(weights),)),
            pltpu.VMEM(start.shape, jnp.float32),
            pltpu.VMEM((count, tokens, depth), jnp.bfloat16),
            pltpu.SemaphoreType.DMA((count,)),
            pltpu.SemaphoreType.DMA((count, 2)),
        ],
        name="near_project",
        **call_options(HEAVY),
    )(start, *rows, *own_rows, *weights)


def near_gradient_kernel(factor, width, stacked, sources_ref, targets_ref, cots, *refs):
    rows, refs = refs[:NX], refs[NX:]
    out = refs[0]
    keys, all_tokens = cots.shape
    tokens = all_tokens // NX
    copies = []
    for j in range(rows[0].shape[1] // width):
        total = None
        for number, row in enumerate(rows):
            left = cots[:, pl.ds(pl.multiple_of(sources_ref[number] * tokens, 128), tokens)]
            term = jnp.dot(
                left, row[:, j * width : (j + 1) * width], preferred_element_type=jnp.float32
            )
            total = term if total is None else total + term
        total = (factor * total).astype(jnp.bfloat16)
        if stacked:
            ready, gone = refs[1:]
            ready[j] = total
            copies.append(
                pltpu.make_async_copy(ready.at[j], out.at[targets_ref[j + 1]], gone.at[j])
            )
            copies[j].start()
        else:
            out[...] = total
    if stacked:
        ready[NY - 1] = jnp.zeros((keys, width), jnp.bfloat16)
        copies.append(
            pltpu.make_async_copy(ready.at[NY - 1], out.at[targets_ref[0]], gone.at[NY - 1])
        )
        copies[NY - 1].start()
    for copy in copies:
        copy.wait()


def near_gradient(sources, targets, cots, rows, width, factor, stacked):
    keys = cots.shape[0]
    shape = (NY, keys, width) if stacked else (keys, width)
    scratch = [pltpu.VMEM(shape, jnp.bfloat16), pltpu.SemaphoreType.DMA((NY,))]
    return pl.pallas_call(
        functools.partial(near_gradient_kernel, factor, width, stacked),
        in_specs=[SMEM, SMEM] + [VMEM] * (1 + NX),
        out_specs=pl.BlockSpec(memory_space=pl.ANY) if stacked else VMEM,
        out_shape=jax.ShapeDtypeStruct(shape, jnp.bfloat16),
        scratch_shapes=scratch if stacked else [],
        name="near_gradient",
        **call_options(HEAVY if stacked else 1, VMEM_LIMIT // 3),
    )(sources, targets, cots, *rows)


def update_kernel(offset_ref, *refs):
    sums_hbm, ins, outs, refs = refs[:4], refs[4:7], refs[7:10], refs[10:]
    weight, first, second, merged, first_new, second_new = refs[:6]
    near, own, far, fresh, came, gone, sums_came = refs[6:]
    rows, keys = weight.shape
    head = fresh.shape[1]
    block = 128
    sums = [
        pltpu.make_async_copy(source, target, sums_came.at[n])
        for n, (source, target) in enumerate(zip(sums_hbm, (near, own, far, fresh)))
    ]
    for copy in sums:
        copy.start()
    fetches, stores = [], []
    for i in range(rows // block):
        span = pl.ds(i * block, block)
        fetches.append(
            [
                pltpu.make_async_copy(source.at[span], target.at[span], came.at[i, n])
                for n, (source, target) in enumerate(zip(ins, (weight, first, second)))
            ]
        )
        stores.append(
            [
                pltpu.make_async_copy(source.at[span], target.at[span], gone.at[i, n])
                for n, (source, target) in enumerate(zip((merged, first_new, second_new), outs))
            ]
        )
        for copy in fetches[i]:
            copy.start()
    for copy in sums:
        copy.wait()
    for i in range(rows // block):
        low, high = i * block, (i + 1) * block
        summed = own[:, low:high].astype(jnp.float32) + far[:, low:high].astype(jnp.float32)
        for number in range(near.shape[0]):
            summed = summed + near[number, :, low:high].astype(jnp.float32)
        gradient = summed.T
        for copy in fetches[i]:
            copy.wait()
        moment_one = beta_one * first[low:high, :] + (1.0 - beta_one) * gradient
        moment_two = beta_two * second[low:high, :] + (1.0 - beta_two) * gradient * gradient
        first_new[low:high, :] = moment_one
        second_new[low:high, :] = moment_two
        master = weight[low:high, :].astype(jnp.float32)
        stepped = master - inner_rate * (
            moment_one / (jnp.sqrt(moment_two) + adam_epsilon) + decay_rate * master
        )
        for position in range(keys // head):
            span = slice(position * head, (position + 1) * head)
            part = stepped[:, span]
            blended = mix_weight * part + (1.0 - mix_weight) * fresh[low:high, :]
            merged[low:high, span] = jnp.where(
                offset_ref[0] == position, blended, part
            ).astype(jnp.bfloat16)
        for copy in stores[i]:
            copy.start()
    for copies in stores:
        for copy in copies:
            copy.wait()


def update(head_index, terms, weight, first, second, fresh):
    rows, keys = weight.shape
    types = [jnp.bfloat16, jnp.float32, jnp.float32]
    return pl.pallas_call(
        update_kernel,
        in_specs=[SMEM] + in_memory(7),
        out_specs=in_memory(3),
        out_shape=[jax.ShapeDtypeStruct((rows, keys), t) for t in types],
        scratch_shapes=[pltpu.VMEM((rows, keys), t) for t in types + types]
        + [pltpu.VMEM(term.shape, term.dtype) for term in (*terms, fresh)]
        + [pltpu.SemaphoreType.DMA((rows // 128, 3))] * 2
        + [pltpu.SemaphoreType.DMA((4,))],
        name="update",
        **call_options(),
    )(head_index, *terms, fresh, weight, first, second)


def per_device(
    activations,
    norm_gain,
    key_cotangent,
    key_weight,
    adam_first,
    adam_second,
    outer_codes,
    outer_scales,
    global_fragment,
    outer_momentum,
    fragment_index,
):
    token_rows = activations[0]
    weight_shard = key_weight[0]
    features = token_rows.shape[1]
    factor = features ** (-0.5)
    width = weight_shard.shape[0]
    replicas = lax.axis_size("replica")

    def swap_x(value):
        return lax.all_to_all(value, "fsdp", 0, 0, axis_index_groups=along_x, tiled=True)

    def add_replica(value, step):
        return value + lax.ppermute(value, "replica", [(r, r ^ step) for r in range(replicas)])

    me = lax.axis_index("fsdp")
    my_y, my_x, my_z = me // (NX * NZ), (me // NZ) % NX, me % NZ

    along_y = [[place(y, x, z) for y in range(NY)] for x in range(NX) for z in range(NZ)]
    along_x = [[place(y, x, z) for x in range(NX)] for y in range(NY) for z in range(NZ)]

    def swap_x(value):
        return lax.all_to_all(value, "fsdp", 0, 0, axis_index_groups=along_x, tiled=True)

    def swap_x(value):
        return lax.all_to_all(value, "fsdp", 0, 0, axis_index_groups=along_x, tiled=True)

    gain = norm_gain.reshape(-1, 128)
    cot = key_cotangent[0]
    keys = cot.shape[1]
    sources = jnp.stack([(my_x - d) % NX for d in range(NX)]).astype(jnp.int32)
    targets = jnp.stack([(my_y + e) % NY for e in range(NY)]).astype(jnp.int32)

    groups = [[(e, 1) for e in range(NY)]]
    (part_one,) = normalize(token_rows, gain, cot, groups, False, width, keys)
    chunk_one = swap_x(part_one)

    near_weights = [weight_shard] + [shift(weight_shard, -e, 0, 0) for e in range(1, NY)]
    far_weight = shift(weight_shard, 0, 0, 1)
    delta = outer_codes[0].astype(jnp.float32) * outer_scales[0].astype(jnp.float32)[:, None]
    delta = add_replica(delta, 1)

    token_rows, far_weight, delta, near_weights = lax.optimization_barrier(
        (token_rows, far_weight, delta, near_weights)
    )
    groups = [[(e, 0) for e in range(1, NY)], [(0, 0)]]
    part_two = normalize(token_rows, gain, cot, groups, True, width, 0)
    part_two, part_own = part_two[:NX], part_two[NX:]
    far_weights = [far_weight] + [shift(far_weight, -e, 0, 0) for e in range(1, NY)]
    delta = add_replica(add_replica(delta, 2), 4)
    chunk_two = [part_two[0]] + [shift(part_two[d], 0, d, 0) for d in range(1, NX)]
    chunk_one, part_two, far_weights, delta = lax.optimization_barrier(
        (chunk_one, part_two, far_weights, delta)
    )

    far, cots = far_gradient(targets, chunk_one, keys, width, factor)
    far = lax.all_to_all(far, "fsdp", 0, 0, axis_index_groups=along_y, tiled=True)
    partial = far_project(sources, chunk_one, far_weights)
    part_own, cots = lax.optimization_barrier((part_own, cots))
    chunk_own = [part_own[0]] + [shift(part_own[d], 0, d, 0) for d in range(1, NX)]
    near = near_gradient(sources, targets, cots, chunk_two, width, factor, True)
    far, near, partial = lax.optimization_barrier((far, near, partial))
    far = shift(add_up(far), 0, 0, 1)
    near = lax.all_to_all(near, "fsdp", 0, 0, axis_index_groups=along_y, tiled=True)

    own_part, *back = near_project(
        partial,
        chunk_two,
        chunk_own,
        near_weights[1:] + [weight_shard],
        [jnp.float32] + [jnp.bfloat16] * (NX - 1),
        factor,
    )
    own = near_gradient(sources, targets, cots, chunk_own, width, factor, False)
    terms = [near, own, far]
    back = [shift(back[d - 1], 0, -d, 0) for d in range(1, NX)]

    outer_delta = delta / replicas
    momentum = outer_beta * outer_momentum + outer_delta
    refreshed = global_fragment - outer_rate * (outer_delta + outer_beta * momentum)

    heads = weight_shard.shape[1] // global_fragment.shape[1]
    head_index = jnp.remainder(fragment_index, heads).astype(jnp.int32)
    merged, moment_one, moment_two = update(
        head_index,
        terms,
        weight_shard,
        adam_first[0],
        adam_second[0],
        refreshed,
    )
    own_part, moment_one = lax.optimization_barrier((own_part, moment_one))
    projected = (own_part + sum(b.astype(jnp.float32) for b in back)).astype(jnp.bfloat16)
    return (
        projected[None],
        merged[None],
        moment_one[None],
        moment_two[None],
        momentum,
        refreshed,
    )


def solution(mesh):
    in_specs = (
        P("replica", "fsdp", None),
        P(),
        P("replica", "fsdp", None),
        P("replica", "fsdp", None),
        P("replica", "fsdp", None),
        P("replica", "fsdp", None),
        P("replica", "fsdp", None),
        P("replica", "fsdp"),
        P("fsdp", None),
        P("fsdp", None),
        P(),
    )
    out_specs = (
        P("replica", "fsdp", None),
        P("replica", "fsdp", None),
        P("replica", "fsdp", None),
        P("replica", "fsdp", None),
        P("fsdp", None),
        P("fsdp", None),
    )
    return jax.shard_map(
        per_device, mesh=mesh, in_specs=in_specs, out_specs=out_specs, check_vma=False
    )
```

```python
import functools

import jax
import jax.numpy as jnp
from jax import lax
from jax.experimental import pallas as pl
from jax.experimental.pallas import tpu as pltpu
from jax.sharding import PartitionSpec as P

norm_epsilon = 1e-05
adam_epsilon = 1e-08
beta_one = 0.9
beta_two = 0.95
inner_rate = 0.02
decay_rate = 0.1
outer_beta = 0.9
outer_rate = 0.7
mix_weight = 0.5

NY, NX, NZ = 4, 4, 2
ROWS = 32
AHEAD = 7
VMEM_LIMIT = 60 * 1024 * 1024
HEAVY = 10**11


def place(y, x, z):
    return ((y % NY) * NX + x % NX) * NZ + z % NZ


def shift(value, dy, dx, dz):
    pairs = [
        (place(y, x, z), place(y + dy, x + dx, z + dz))
        for y in range(NY)
        for x in range(NX)
        for z in range(NZ)
    ]
    return lax.ppermute(value, "fsdp", pairs)


def in_memory(count):
    return [pl.BlockSpec(memory_space=pl.ANY)] * count


def call_options(work=1, limit=VMEM_LIMIT):
    return dict(
        compiler_params=pltpu.CompilerParams(vmem_limit_bytes=limit),
        cost_estimate=pl.CostEstimate(flops=work, bytes_accessed=1, transcendentals=0),
    )


def norm_kernel(width, groups, relative, extra, rows_hbm, gain_ref, cot_hbm, *refs):
    outs, (held, ready, cot, gains, came, gone, cot_came, cot_gone) = refs[:-8], refs[-8:]
    tokens, features = held.shape
    blocks = [block for group in groups for block in group]
    lanes = 128
    bands = tokens // ROWS
    me = lax.axis_index("fsdp")
    my_y, my_x, my_z = me // (NX * NZ), (me // NZ) % NX, me % NZ

    def fetch(band):
        rows = pl.ds(pl.multiple_of(band * ROWS, ROWS), ROWS)
        return pltpu.make_async_copy(rows_hbm.at[rows], held.at[rows], came.at[band])

    def stores(band, x):
        rows = pl.ds(pl.multiple_of(band * ROWS, ROWS), ROWS)
        low, copies = 0, []
        for number, group in enumerate(groups):
            span = pl.ds(low, width * len(group))
            if relative:
                target = outs[number * NX + x].at[rows]
            else:
                target = outs[number].at[x, rows, span]
            copies.append(
                pltpu.make_async_copy(ready.at[x, rows, span], target, gone.at[band, x, number])
            )
            low += width * len(group)
        return copies

    for band in range(AHEAD):
        fetch(band).start()
    cot_copies = []
    if extra:
        cot_fetch = pltpu.make_async_copy(cot_hbm, cot, cot_came)
        cot_fetch.start()
        cot_copies = [
            pltpu.make_async_copy(cot, outs[0].at[x, :, pl.ds(width * len(blocks), extra)], cot_gone.at[x])
            for x in range(NX)
        ]
    gains[...] = gain_ref[...].astype(jnp.float32)
    starts = [
        [
            place(my_y + y, (my_x if relative else 0) + x, my_z + z) * (width // lanes)
            for y, z in blocks
        ]
        for x in range(NX)
    ]

    @pl.loop(0, bands)
    def _(band):
        @pl.when(band + AHEAD < bands)
        def _():
            fetch(band + AHEAD).start()

        fetch(band).wait()
        rows = pl.ds(pl.multiple_of(band * ROWS, ROWS), ROWS)
        sums = [jnp.zeros((ROWS, lanes), jnp.float32) for _ in range(2)]
        for k in range(features // lanes):
            part = held[rows, k * lanes : (k + 1) * lanes].astype(jnp.float32)
            sums[k % 2] = sums[k % 2] + part * part
        total = jnp.sum(sums[0] + sums[1], axis=1, keepdims=True)
        scale = lax.rsqrt(total / features + norm_epsilon)
        scale = jnp.broadcast_to(scale, (ROWS, lanes))
        for x in range(NX):
            for position in range(len(blocks)):
                for k in range(width // lanes):
                    tile = starts[x][position] + k
                    column = pl.multiple_of(tile * lanes, lanes)
                    part = held[rows, pl.ds(column, lanes)].astype(jnp.float32)
                    gain = gains[pl.ds(tile, 1), :]
                    low = position * width + k * lanes
                    ready[x, rows, low : low + lanes] = (part * scale * gain).astype(jnp.bfloat16)
            for copy in stores(band, x):
                copy.start()

    if extra:
        cot_fetch.wait()
        for copy in cot_copies:
            copy.start()
        for copy in cot_copies:
            copy.wait()
    for band in range(bands):
        for x in range(NX):
            for copy in stores(band, x):
                copy.wait()


def normalize(token_rows, gain, cot, groups, relative, width, extra):
    tokens, features = token_rows.shape
    depths = [width * len(group) for group in groups]
    bands = tokens // ROWS
    if relative:
        out_shape = [
            jax.ShapeDtypeStruct((tokens, depth), jnp.bfloat16) for depth in depths for _ in range(NX)
        ]
    else:
        out_shape = [jax.ShapeDtypeStruct((NX, tokens, depths[0] + extra), jnp.bfloat16)]
    return pl.pallas_call(
        functools.partial(norm_kernel, width, groups, relative, extra),
        in_specs=[
            pl.BlockSpec(memory_space=pl.ANY),
            pl.BlockSpec(memory_space=pltpu.VMEM),
            pl.BlockSpec(memory_space=pl.ANY),
        ],
        out_specs=in_memory(len(out_shape)),
        out_shape=out_shape,
        scratch_shapes=[
            pltpu.VMEM((tokens, features), jnp.bfloat16),
            pltpu.VMEM((NX, tokens, sum(depths)), jnp.bfloat16),
            pltpu.VMEM(cot.shape, jnp.bfloat16),
            pltpu.VMEM(gain.shape, jnp.float32),
            pltpu.SemaphoreType.DMA((bands,)),
            pltpu.SemaphoreType.DMA((bands, NX, len(groups))),
            pltpu.SemaphoreType.DMA,
            pltpu.SemaphoreType.DMA((NX,)),
        ],
        name="norm",
        **call_options(),
    )(token_rows, gain, cot)


VMEM = pl.BlockSpec(memory_space=pltpu.VMEM)
SMEM = pl.BlockSpec(memory_space=pltpu.SMEM)


def far_gradient_kernel(factor, width, targets_ref, chunk, far_hbm, cots, ready, gone):
    sources, tokens, depth = chunk.shape
    keys = cots.shape[0]
    for source in range(sources):
        cots[:, source * tokens : (source + 1) * tokens] = chunk[source, :, depth - keys :].T
    copies = []
    for j in range(NY):
        total = None
        for source in range(sources):
            term = jnp.dot(
                cots[:, source * tokens : (source + 1) * tokens],
                chunk[source, :, j * width : (j + 1) * width],
                preferred_element_type=jnp.float32,
            )
            total = term if total is None else total + term
        ready[j] = (factor * total).astype(jnp.bfloat16)
        copies.append(
            pltpu.make_async_copy(ready.at[j], far_hbm.at[targets_ref[j]], gone.at[j])
        )
        copies[j].start()
    for copy in copies:
        copy.wait()


def far_gradient(targets, chunk, keys, width, factor):
    sources, tokens, _ = chunk.shape
    return pl.pallas_call(
        functools.partial(far_gradient_kernel, factor, width),
        in_specs=[SMEM, VMEM],
        out_specs=[pl.BlockSpec(memory_space=pl.ANY), VMEM],
        out_shape=[
            jax.ShapeDtypeStruct((NY, keys, width), jnp.bfloat16),
            jax.ShapeDtypeStruct((keys, sources * tokens), jnp.bfloat16),
        ],
        scratch_shapes=[
            pltpu.VMEM((NY, keys, width), jnp.bfloat16),
            pltpu.SemaphoreType.DMA((NY,)),
        ],
        name="far_gradient",
        **call_options(HEAVY, VMEM_LIMIT // 3),
    )(targets, chunk)


def add_up_kernel(terms, out):
    total = terms[0].astype(jnp.float32)
    for number in range(1, terms.shape[0]):
        total = total + terms[number].astype(jnp.float32)
    out[...] = total.astype(out.dtype)


def add_up(terms):
    return pl.pallas_call(
        add_up_kernel,
        in_specs=[VMEM],
        out_specs=VMEM,
        out_shape=jax.ShapeDtypeStruct(terms.shape[1:], terms.dtype),
        name="add_up",
        **call_options(1, VMEM_LIMIT // 3),
    )(terms)


def fetch_weights(weights_hbm, weights, came):
    width = weights.shape[0] // len(weights_hbm)
    copies = [
        pltpu.make_async_copy(weight, weights.at[pl.ds(j * width, width)], came.at[j])
        for j, weight in enumerate(weights_hbm)
    ]
    for copy in copies:
        copy.start()
    return copies


def far_project_kernel(sources_ref, chunk, *refs):
    weights_hbm, (out, weights, came, ready, gone) = refs[:-5], refs[-5:]
    for copy in fetch_weights(weights_hbm, weights, came):
        copy.wait()
    copies = []
    for d in range(NX):
        ready[d] = jnp.dot(
            chunk[sources_ref[d], :, : weights.shape[0]],
            weights[...],
            preferred_element_type=jnp.float32,
        )
        copies.append(pltpu.make_async_copy(ready.at[d], out.at[d], gone.at[d]))
        copies[d].start()
    for copy in copies:
        copy.wait()


def far_project(sources, chunk, weights):
    count, tokens, _ = chunk.shape
    width, keys = weights[0].shape
    shape = (count, tokens, keys)
    return pl.pallas_call(
        far_project_kernel,
        in_specs=[SMEM, VMEM] + in_memory(len(weights)),
        out_specs=pl.BlockSpec(memory_space=pl.ANY),
        out_shape=jax.ShapeDtypeStruct(shape, jnp.float32),
        scratch_shapes=[
            pltpu.VMEM((width * len(weights), keys), jnp.bfloat16),
            pltpu.SemaphoreType.DMA((len(weights),)),
            pltpu.VMEM(shape, jnp.float32),
            pltpu.SemaphoreType.DMA((count,)),
        ],
        name="far_project",
        **call_options(HEAVY, VMEM_LIMIT // 3),
    )(sources, chunk, *weights)


def near_project_kernel(factor, pieces, start_hbm, *refs):
    rows_hbm, own_hbm, refs = refs[:NX], refs[NX : 2 * NX], refs[2 * NX :]
    weights_hbm, refs = refs[:pieces], refs[pieces:]
    outs, (weights, came, start, rows, start_came, rows_came) = refs[:NX], refs[NX:]
    depth = rows_hbm[0].shape[1]
    own_depth = own_hbm[0].shape[1]
    copies = fetch_weights(weights_hbm, weights, came)
    fetches = []
    for d in range(NX):
        fetches.append(
            [
                pltpu.make_async_copy(
                    rows_hbm[d], rows.at[d, :, pl.ds(0, depth)], rows_came.at[d, 0]
                ),
                pltpu.make_async_copy(
                    own_hbm[d], rows.at[d, :, pl.ds(depth, own_depth)], rows_came.at[d, 1]
                ),
                pltpu.make_async_copy(start_hbm.at[d], start.at[d], start_came.at[d]),
            ]
        )
        for copy in fetches[d]:
            copy.start()
    for copy in copies:
        copy.wait()
    for d in range(NX):
        for copy in fetches[d]:
            copy.wait()
        total = start[d] + jnp.dot(rows[d], weights[...], preferred_element_type=jnp.float32)
        outs[d][...] = (factor * total).astype(outs[d].dtype)


def near_project(start, rows, own_rows, weights, out_types, factor):
    width, keys = weights[0].shape
    count, tokens, _ = start.shape
    depth = width * len(weights)
    return pl.pallas_call(
        functools.partial(near_project_kernel, factor, len(weights)),
        in_specs=in_memory(1 + 2 * NX + len(weights)),
        out_specs=[VMEM] * NX,
        out_shape=[jax.ShapeDtypeStruct((tokens, keys), t) for t in out_types],
        scratch_shapes=[
            pltpu.VMEM((depth, keys), jnp.bfloat16),
            pltpu.SemaphoreType.DMA((len(weights),)),
            pltpu.VMEM(start.shape, jnp.float32),
            pltpu.VMEM((count, tokens, depth), jnp.bfloat16),
            pltpu.SemaphoreType.DMA((count,)),
            pltpu.SemaphoreType.DMA((count, 2)),
        ],
        name="near_project",
        **call_options(HEAVY),
    )(start, *rows, *own_rows, *weights)


def near_gradient_kernel(factor, width, stacked, sources_ref, targets_ref, cots, *refs):
    rows, refs = refs[:NX], refs[NX:]
    out = refs[0]
    keys, all_tokens = cots.shape
    tokens = all_tokens // NX
    copies = []
    for j in range(rows[0].shape[1] // width):
        total = None
        for number, row in enumerate(rows):
            left = cots[:, pl.ds(pl.multiple_of(sources_ref[number] * tokens, 128), tokens)]
            term = jnp.dot(
                left, row[:, j * width : (j + 1) * width], preferred_element_type=jnp.float32
            )
            total = term if total is None else total + term
        total = (factor * total).astype(jnp.bfloat16)
        if stacked:
            ready, gone = refs[1:]
            ready[j] = total
            copies.append(
                pltpu.make_async_copy(ready.at[j], out.at[targets_ref[j + 1]], gone.at[j])
            )
            copies[j].start()
        else:
            out[...] = total
    if stacked:
        ready[NY - 1] = jnp.zeros((keys, width), jnp.bfloat16)
        copies.append(
            pltpu.make_async_copy(ready.at[NY - 1], out.at[targets_ref[0]], gone.at[NY - 1])
        )
        copies[NY - 1].start()
    for copy in copies:
        copy.wait()


def near_gradient(sources, targets, cots, rows, width, factor, stacked):
    keys = cots.shape[0]
    shape = (NY, keys, width) if stacked else (keys, width)
    scratch = [pltpu.VMEM(shape, jnp.bfloat16), pltpu.SemaphoreType.DMA((NY,))]
    return pl.pallas_call(
        functools.partial(near_gradient_kernel, factor, width, stacked),
        in_specs=[SMEM, SMEM] + [VMEM] * (1 + NX),
        out_specs=pl.BlockSpec(memory_space=pl.ANY) if stacked else VMEM,
        out_shape=jax.ShapeDtypeStruct(shape, jnp.bfloat16),
        scratch_shapes=scratch if stacked else [],
        name="near_gradient",
        **call_options(HEAVY if stacked else 1, VMEM_LIMIT // 3),
    )(sources, targets, cots, *rows)


def update_kernel(offset_ref, *refs):
    sums_hbm, ins, outs, refs = refs[:4], refs[4:7], refs[7:10], refs[10:]
    weight, first, second, merged, first_new, second_new = refs[:6]
    near, own, far, fresh, came, gone, sums_came = refs[6:]
    rows, keys = weight.shape
    head = fresh.shape[1]
    block = 128
    fetches, stores = [], []
    for i in range(rows // block):
        span = pl.ds(i * block, block)
        fetches.append(
            [
                pltpu.make_async_copy(source.at[span], target.at[span], came.at[i, n])
                for n, (source, target) in enumerate(zip(ins, (weight, first, second)))
            ]
            + [
                pltpu.make_async_copy(
                    sums_hbm[0].at[:, :, span], near.at[:, :, span], sums_came.at[i, 0]
                ),
                pltpu.make_async_copy(
                    sums_hbm[1].at[:, span], own.at[:, span], sums_came.at[i, 1]
                ),
                pltpu.make_async_copy(
                    sums_hbm[2].at[:, span], far.at[:, span], sums_came.at[i, 2]
                ),
                pltpu.make_async_copy(sums_hbm[3].at[span], fresh.at[span], sums_came.at[i, 3]),
            ]
        )
        stores.append(
            [
                pltpu.make_async_copy(source.at[span], target.at[span], gone.at[i, n])
                for n, (source, target) in enumerate(zip((merged, first_new, second_new), outs))
            ]
        )
        for copy in fetches[i]:
            copy.start()
    for i in range(rows // block):
        low, high = i * block, (i + 1) * block
        for copy in fetches[i]:
            copy.wait()
        summed = own[:, low:high].astype(jnp.float32) + far[:, low:high].astype(jnp.float32)
        for number in range(near.shape[0]):
            summed = summed + near[number, :, low:high].astype(jnp.float32)
        gradient = summed.T
        moment_one = beta_one * first[low:high, :] + (1.0 - beta_one) * gradient
        moment_two = beta_two * second[low:high, :] + (1.0 - beta_two) * gradient * gradient
        first_new[low:high, :] = moment_one
        second_new[low:high, :] = moment_two
        master = weight[low:high, :].astype(jnp.float32)
        stepped = master - inner_rate * (
            moment_one / (jnp.sqrt(moment_two) + adam_epsilon) + decay_rate * master
        )
        for position in range(keys // head):
            span = slice(position * head, (position + 1) * head)
            part = stepped[:, span]
            blended = mix_weight * part + (1.0 - mix_weight) * fresh[low:high, :]
            merged[low:high, span] = jnp.where(
                offset_ref[0] == position, blended, part
            ).astype(jnp.bfloat16)
        for copy in stores[i]:
            copy.start()
    for copies in stores:
        for copy in copies:
            copy.wait()


def update(head_index, terms, weight, first, second, fresh):
    rows, keys = weight.shape
    types = [jnp.bfloat16, jnp.float32, jnp.float32]
    return pl.pallas_call(
        update_kernel,
        in_specs=[SMEM] + in_memory(7),
        out_specs=in_memory(3),
        out_shape=[jax.ShapeDtypeStruct((rows, keys), t) for t in types],
        scratch_shapes=[pltpu.VMEM((rows, keys), t) for t in types + types]
        + [pltpu.VMEM(term.shape, term.dtype) for term in (*terms, fresh)]
        + [pltpu.SemaphoreType.DMA((rows // 128, 3))] * 2
        + [pltpu.SemaphoreType.DMA((rows // 128, 4))],
        name="update",
        **call_options(),
    )(head_index, *terms, fresh, weight, first, second)


def per_device(
    activations,
    norm_gain,
    key_cotangent,
    key_weight,
    adam_first,
    adam_second,
    outer_codes,
    outer_scales,
    global_fragment,
    outer_momentum,
    fragment_index,
):
    token_rows = activations[0]
    weight_shard = key_weight[0]
    features = token_rows.shape[1]
    factor = features ** (-0.5)
    width = weight_shard.shape[0]
    replicas = lax.axis_size("replica")

    def swap_x(value):
        return lax.all_to_all(value, "fsdp", 0, 0, axis_index_groups=along_x, tiled=True)

    def add_replica(value, step):
        return value + lax.ppermute(value, "replica", [(r, r ^ step) for r in range(replicas)])

    me = lax.axis_index("fsdp")
    my_y, my_x, my_z = me // (NX * NZ), (me // NZ) % NX, me % NZ

    along_y = [[place(y, x, z) for y in range(NY)] for x in range(NX) for z in range(NZ)]
    along_x = [[place(y, x, z) for x in range(NX)] for y in range(NY) for z in range(NZ)]

    def swap_x(value):
        return lax.all_to_all(value, "fsdp", 0, 0, axis_index_groups=along_x, tiled=True)

    def swap_x(value):
        return lax.all_to_all(value, "fsdp", 0, 0, axis_index_groups=along_x, tiled=True)

    gain = norm_gain.reshape(-1, 128)
    cot = key_cotangent[0]
    keys = cot.shape[1]
    sources = jnp.stack([(my_x - d) % NX for d in range(NX)]).astype(jnp.int32)
    targets = jnp.stack([(my_y + e) % NY for e in range(NY)]).astype(jnp.int32)

    groups = [[(e, 1) for e in range(NY)]]
    (part_one,) = normalize(token_rows, gain, cot, groups, False, width, keys)
    chunk_one = swap_x(part_one)

    near_weights = [weight_shard] + [shift(weight_shard, -e, 0, 0) for e in range(1, NY)]
    far_weight = shift(weight_shard, 0, 0, 1)
    delta = outer_codes[0].astype(jnp.float32) * outer_scales[0].astype(jnp.float32)[:, None]
    delta = add_replica(delta, 1)

    token_rows, far_weight, delta, near_weights = lax.optimization_barrier(
        (token_rows, far_weight, delta, near_weights)
    )
    groups = [[(e, 0) for e in range(1, NY)], [(0, 0)]]
    part_two = normalize(token_rows, gain, cot, groups, True, width, 0)
    part_two, part_own = part_two[:NX], part_two[NX:]
    far_weights = [far_weight] + [shift(far_weight, -e, 0, 0) for e in range(1, NY)]
    delta = add_replica(add_replica(delta, 2), 4)
    chunk_two = [part_two[0]] + [shift(part_two[d], 0, d, 0) for d in range(1, NX)]
    chunk_one, part_two, far_weights, delta = lax.optimization_barrier(
        (chunk_one, part_two, far_weights, delta)
    )

    far, cots = far_gradient(targets, chunk_one, keys, width, factor)
    far = lax.all_to_all(far, "fsdp", 0, 0, axis_index_groups=along_y, tiled=True)
    partial = far_project(sources, chunk_one, far_weights)
    part_own, cots = lax.optimization_barrier((part_own, cots))
    chunk_own = [part_own[0]] + [shift(part_own[d], 0, d, 0) for d in range(1, NX)]
    near = near_gradient(sources, targets, cots, chunk_two, width, factor, True)
    far, near, partial = lax.optimization_barrier((far, near, partial))
    far = shift(add_up(far), 0, 0, 1)
    near = lax.all_to_all(near, "fsdp", 0, 0, axis_index_groups=along_y, tiled=True)

    own_part, *back = near_project(
        partial,
        chunk_two,
        chunk_own,
        near_weights[1:] + [weight_shard],
        [jnp.float32] + [jnp.bfloat16] * (NX - 1),
        factor,
    )
    own = near_gradient(sources, targets, cots, chunk_own, width, factor, False)
    terms = [near, own, far]
    back = [shift(back[d - 1], 0, -d, 0) for d in range(1, NX)]

    outer_delta = delta / replicas
    momentum = outer_beta * outer_momentum + outer_delta
    refreshed = global_fragment - outer_rate * (outer_delta + outer_beta * momentum)

    heads = weight_shard.shape[1] // global_fragment.shape[1]
    head_index = jnp.remainder(fragment_index, heads).astype(jnp.int32)
    merged, moment_one, moment_two = update(
        head_index,
        terms,
        weight_shard,
        adam_first[0],
        adam_second[0],
        refreshed,
    )
    own_part, moment_one = lax.optimization_barrier((own_part, moment_one))
    projected = (own_part + sum(b.astype(jnp.float32) for b in back)).astype(jnp.bfloat16)
    return (
        projected[None],
        merged[None],
        moment_one[None],
        moment_two[None],
        momentum,
        refreshed,
    )


def solution(mesh):
    in_specs = (
        P("replica", "fsdp", None),
        P(),
        P("replica", "fsdp", None),
        P("replica", "fsdp", None),
        P("replica", "fsdp", None),
        P("replica", "fsdp", None),
        P("replica", "fsdp", None),
        P("replica", "fsdp"),
        P("fsdp", None),
        P("fsdp", None),
        P(),
    )
    out_specs = (
        P("replica", "fsdp", None),
        P("replica", "fsdp", None),
        P("replica", "fsdp", None),
        P("replica", "fsdp", None),
        P("fsdp", None),
        P("fsdp", None),
    )
    return jax.shard_map(
        per_device, mesh=mesh, in_specs=in_specs, out_specs=out_specs, check_vma=False
    )
```
